256 devices in a mesh: fsdp: 128 (over x_lo, z, y, core), opt: 2 (over x_hi).
Axes of the slice: x: 4 (x_hi: 2, x_lo: 2; x = x_hi * 2 + x_lo), y: 4, z: 8, core: 2. Of those that a mesh axis runs over, the one named last changes fastest.
Arguments:
- gradient: bfloat16 [16384, 16384], P(('fsdp', 'opt')), may hold values from -200 to 200
- momentum: float32 [128, 2, 2048, 4, 128], P('fsdp', 'opt'), may hold values from -200 to 200
- head_order: int32 [128], replicated, may hold values from 0 to 127, each once
Outputs:
- update: bfloat16 [16384, 16384], P(('fsdp', 'opt'))
- new_momentum: float32 [128, 2, 2048, 4, 128], P('fsdp', 'opt')
The draws below stay inside these ranges and needn't reach their ends.
Inputs may be any that keep to these rules, and one draw needn't show every extreme that they name: `head_order`: each of 0 to 127 appears once.
All inputs are finite; a program needn't handle non-finite values.
Results may differ from the reference program's by a relative error of at most 0.001.
Values may be sent and summed in bfloat16 or wider, within the bound.
A program may use at most 128 MiB of HBM per device.

```python
import math
import jax
import jax.numpy as jnp
from jax import lax

D = 16384
HD = 128
BPG = 4
ROW_SPLIT = 8
ITERS = 5
BLOCKS = 128
N_FSDP = 128
N_OPT = 2


def draw_gradient(key, part):
    key = jax.random.fold_in(key, 11)
    key_base, key_row, key_col = jax.random.split(key, 3)
    shape = (D, BLOCKS * HD)
    row_index = (jnp.arange(D, dtype=jnp.int32) % ROW_SPLIT).astype(jnp.float32)
    trend = 3.0 ** (row_index / (ROW_SPLIT - 1))
    base = jnp.clip(jax.random.normal(key_base, shape, jnp.float32), -4.0, 4.0)
    row_scale = jnp.exp(jax.random.uniform(key_row, (D,), jnp.float32, 0.0, math.log(10.0)))
    col_scale = jnp.exp(jax.random.uniform(key_col, (BLOCKS * HD,), jnp.float32, 0.0, math.log(10.0)))
    values = 0.1 * base * (trend * row_scale)[:, None] * col_scale[None, :]
    return values.astype(jnp.bfloat16)


def draw_momentum(key, part):
    key = jax.random.fold_in(key, 23)
    key_base, key_row, key_col = jax.random.split(key, 3)
    shape = (N_FSDP, N_OPT, D // ROW_SPLIT, BPG, HD)
    device_index = (jnp.arange(N_FSDP, dtype=jnp.int32) % ROW_SPLIT).astype(jnp.float32)
    trend = (3.0 ** (device_index / (ROW_SPLIT - 1))).reshape(N_FSDP, 1, 1, 1, 1)
    row_shape = (N_FSDP, N_OPT, D // ROW_SPLIT, BPG, 1)
    base = jnp.clip(jax.random.normal(key_base, shape, jnp.float32), -4.0, 4.0)
    row_scale = jnp.exp(jax.random.uniform(key_row, row_shape, jnp.float32, 0.0, math.log(10.0)))
    col_scale = jnp.exp(jax.random.uniform(key_col, (1, N_OPT, 1, BPG, HD), jnp.float32, 0.0, math.log(10.0)))
    return 0.1 * base * trend * row_scale * col_scale


def setup_inputs(seed: int = 0) -> dict:
    key_of = jax.random.split(jax.random.key(seed), 4)
    return {
        "gradient": draw_gradient(jax.random.fold_in(key_of[3], 71), 0),
        "momentum": draw_momentum(jax.random.fold_in(key_of[3], 71), 0),
        "head_order": jax.random.permutation(key_of[2], BLOCKS).astype(jnp.int32),
    }


decay_rate = 0.95
first_coeff = 3.4445
second_coeff = -4.775
third_coeff = 2.0315
epsilon = 1e-07
gain_factor = 0.2

def matmul_high(left, right):
    return jnp.dot(left, right, precision=lax.Precision.HIGHEST, preferred_element_type=jnp.float32)

def orthogonal(nesterov):
    sq_norm = jnp.sum(nesterov * nesterov)
    iterate = nesterov / (jnp.sqrt(sq_norm) + epsilon)
    for step in range(ITERS):
        gram_now = matmul_high(iterate.T, iterate)
        poly_term = second_coeff * gram_now + third_coeff * matmul_high(gram_now, gram_now)
        iterate = first_coeff * iterate + matmul_high(iterate, poly_term)
    return iterate

def reference(gradient, momentum, head_order):
    blocks = head_order.shape[0]
    groups = N_FSDP // ROW_SPLIT
    source_of = jnp.argsort(head_order).astype(jnp.int32)
    by_block = gradient.reshape(D, blocks, HD)
    state = momentum.reshape(groups, ROW_SPLIT, N_OPT, D // ROW_SPLIT, BPG, HD)
    state = state.transpose(2, 0, 4, 3, 1, 5).reshape(blocks, D, HD)
    gain_total = gain_factor * math.sqrt(max(D, HD))

    def one_block(index):
        grad_block = lax.dynamic_index_in_dim(by_block, source_of[index], 1, keepdims=False).astype(jnp.float32)
        old_block = lax.dynamic_index_in_dim(state, index, 0, keepdims=False)
        new_block = decay_rate * old_block + grad_block
        nesterov = grad_block + decay_rate * new_block
        result = (gain_total * orthogonal(nesterov)).astype(jnp.bfloat16)
        return (new_block, result)
    new_state, updates = lax.map(one_block, jnp.arange(blocks, dtype=jnp.int32))
    new_state = new_state.reshape(N_OPT, groups, BPG, D // ROW_SPLIT, ROW_SPLIT, HD)
    new_state = new_state.transpose(1, 4, 0, 3, 2, 5).reshape(N_FSDP, N_OPT, D // ROW_SPLIT, BPG, HD)
    placed = jnp.take(updates, head_order, axis=0)
    placed = placed.transpose(1, 0, 2).reshape(D, blocks * HD)
    return (placed, new_state)
```

```python
import math

import jax
import jax.numpy as jnp
from jax import lax
from jax.sharding import PartitionSpec as P

D = 16384
HD = 128
BPG = 4
ROW_SPLIT = 8
ITERS = 5


decay_rate = 0.95
first_coeff = 3.4445
second_coeff = -4.775
third_coeff = 2.0315
epsilon = 1e-07
gain_factor = 0.2


def partner(value, axis, apart):
    mask = 2**apart
    pairs = [(source, source ^ mask) for source in range(lax.axis_size(axis))]
    return lax.ppermute(value, axis, pairs)


def batched(left, right):
    return jnp.einsum("jab,jbc->jac", left, right, precision=lax.Precision.HIGHEST)


def local_gram(values):
    return jnp.einsum("rjc,rjd->jcd", values, values, precision=lax.Precision.HIGHEST)


def gram_sum(partial_value):
    summed = partial_value
    for bit_index in range(ROW_SPLIT.bit_length() - 1):
        summed = summed + partner(summed, "fsdp", bit_index)
    return summed


def per_device(gradient, momentum, head_order):
    fsdp_size = lax.axis_size("fsdp")
    opt_size = lax.axis_size("opt")
    groups = fsdp_size // ROW_SPLIT
    blocks = head_order.shape[0]
    head_size = HD
    src_rows = gradient.shape[0]
    inner = src_rows // ROW_SPLIT
    positions = jnp.arange(blocks, dtype=jnp.int32)
    source_of = jnp.sum(
        jnp.where(head_order[:, None] == positions[None, :], positions[:, None], 0), axis=0
    )
    by_block = jnp.take(gradient.reshape(src_rows, blocks, head_size), source_of, axis=1)
    sectioned = by_block.reshape(inner, ROW_SPLIT, opt_size, groups, BPG, head_size)
    sectioned = sectioned.transpose(3, 1, 2, 0, 4, 5).reshape(
        fsdp_size * opt_size, inner, BPG * head_size
    )
    arrived = lax.all_to_all(sectioned, ("fsdp", "opt"), split_axis=0, concat_axis=0, tiled=True)
    local_grad = arrived.reshape(-1, BPG, head_size).astype(jnp.float32)
    previous = momentum.reshape(-1, BPG, head_size)
    new_state = decay_rate * previous + local_grad
    nesterov = local_grad + decay_rate * new_state
    gram_now = gram_sum(local_gram(nesterov))
    sq_norm = jnp.trace(gram_now, axis1=1, axis2=2)
    inv_norm = (1.0 / (jnp.sqrt(sq_norm) + epsilon))[:, None, None]
    gram_now = gram_now * inv_norm * inv_norm
    gain_total = gain_factor * math.sqrt(max(D, HD))
    eye = jnp.eye(head_size, dtype=jnp.float32)
    chain = None
    for step in range(ITERS):
        factor = first_coeff * eye + second_coeff * gram_now + third_coeff * batched(gram_now, gram_now)
        chain = factor if chain is None else batched(chain, factor)
        if step < ITERS - 1:
            gram_now = batched(factor, batched(gram_now, factor))
    chain = chain * (gain_total * inv_norm)
    result = jnp.einsum("rjc,jcd->rjd", nesterov, chain, precision=lax.Precision.HIGHEST)
    result = result.astype(jnp.bfloat16)
    outgoing = result.reshape(fsdp_size * opt_size, inner, BPG * head_size)
    returned = lax.all_to_all(outgoing, ("fsdp", "opt"), split_axis=0, concat_axis=0, tiled=True)
    returned = returned.reshape(groups, ROW_SPLIT, opt_size, inner, BPG, head_size)
    returned = returned.transpose(3, 1, 2, 0, 4, 5).reshape(src_rows, blocks, head_size)
    placed = jnp.take(returned, head_order, axis=1).reshape(src_rows, blocks * head_size)
    return (placed, new_state.reshape(momentum.shape))


def solution(mesh):
    in_specs = (P(("fsdp", "opt"), None), P("fsdp", "opt", None, None, None), P())
    out_specs = (P(("fsdp", "opt"), None), P("fsdp", "opt", None, None, None))
    return jax.shard_map(
        per_device, mesh=mesh, in_specs=in_specs, out_specs=out_specs, check_vma=False
    )
```

```python
import math

import jax
import jax.numpy as jnp
from jax import lax
from jax.experimental import pallas as pl
from jax.experimental.pallas import tpu as pltpu
from jax.sharding import PartitionSpec as P

D = 16384
HD = 128
BPG = 4
ROW_SPLIT = 8
ITERS = 5
NX, NY, NZ, NCORE = 4, 4, 8, 2
NDEV = NX * NY * NZ * NCORE
SUB = 8
CHUNK = SUB * BPG
BATCH = NX * ROW_SPLIT
ROWS = NDEV * CHUNK

decay_rate = 0.95
first_coeff = 3.4445
second_coeff = -4.775
third_coeff = 2.0315
epsilon = 1e-07
gain_factor = 0.2

MESH = pl.DeviceIdType.MESH
HIGHEST = lax.Precision.HIGHEST


def dot(left, right, left_dim=1):
    return lax.dot_general(
        left, right, (((left_dim,), (0,)), ((), ())), precision=HIGHEST, preferred_element_type=jnp.float32
    )


def z_offset(turn):
    back = NZ - 1 - turn
    odd = back % 2
    return odd * ((back + 1) // 2) + (1 - odd) * ((NZ - back // 2) % NZ)


def place(z, x, k):
    return (z * NX + x) * ROW_SPLIT + k, ((x % 2) * NZ + z) * ROW_SPLIT + k, x // 2


def chunk_of(index):
    return pl.ds(pl.multiple_of(index * CHUNK, CHUNK), CHUNK)


def kernel(
    source_ref,
    grad_ref,
    mom_hbm,
    ret_hbm,
    new_hbm,
    mom,
    send,
    recv,
    nest,
    back,
    stage,
    gram,
    gram_in,
    chain,
    send_sem,
    recv_sem,
    back_send_sem,
    back_recv_sem,
    gram_sems,
    chain_sems,
    local_sems,
):
    f, o = lax.axis_index("fsdp"), lax.axis_index("opt")
    my_k = f % ROW_SPLIT
    my_z = (f // ROW_SPLIT) % NZ
    my_x = o * 2 + f // (ROW_SPLIT * NZ)
    my_y, my_core = my_k // 2, my_k % 2
    my_e, _, _ = place(my_z, my_x, my_k)

    mom_in = pltpu.make_async_copy(mom_hbm, mom, local_sems.at[0])
    mom_in.start()

    def target_k(kk):
        return ((my_y + kk // 2) % NY) * 2 + (my_core + kk % 2) % 2

    def send_group(turn, r, own):
        z, x = (my_z + z_offset(turn)) % NZ, (my_x + r) % NX
        group = (x // 2) * 16 + (x % 2) * NZ + z
        for j in range(BPG):
            column = source_ref[group * BPG + j] * HD
            stage[j] = grad_ref[:, pl.ds(column, HD)].astype(jnp.float32)
        for kk in range(ROW_SPLIT):
            k = target_k(kk)
            e, to_f, to_o = place(z, x, k)
            parts = [stage[j, pl.ds(k, SUB, stride=ROW_SPLIT), :] for j in range(BPG)]
            chunk = jnp.concatenate(parts, axis=0).astype(jnp.bfloat16)
            if own and kk == 0:
                recv[chunk_of(my_e), :] = chunk
                continue
            send[chunk_of(e), :] = chunk
            pltpu.make_async_remote_copy(
                src_ref=send.at[chunk_of(e), :],
                dst_ref=recv.at[chunk_of(my_e), :],
                send_sem=send_sem,
                recv_sem=recv_sem.at[turn],
                device_id=(to_f, to_o),
                device_id_type=MESH,
            ).start()

    def send_turn(index, carry):
        send_group(index // NX, index % NX, False)
        return carry

    lax.fori_loop(0, (NZ - 1) * NX, send_turn, 0)
    send_group(NZ - 1, 0, True)

    def send_last(r, carry):
        send_group(NZ - 1, r, False)
        return carry

    lax.fori_loop(1, NX, send_last, 0)

    def waiter(count, ref, one, two):
        whole = ref.at[pl.ds(0, count * CHUNK), :]
        return pltpu.make_async_remote_copy(
            src_ref=whole, dst_ref=whole, send_sem=one, recv_sem=two, device_id=(f, o), device_id_type=MESH
        )

    mom_in.wait()
    gram[...] = jnp.zeros_like(gram)

    def absorb(turn, count):
        waiter(count, recv, send_sem, recv_sem.at[turn]).wait_recv()
        z = (my_z + NZ - z_offset(turn)) % NZ

        def one_chunk(index, carry):
            x, k = index // ROW_SPLIT, index % ROW_SPLIT
            e, from_f, from_o = place(z, x, k)
            value = recv[chunk_of(e), :].astype(jnp.float32)
            first = (from_f * 2 + from_o) * CHUNK
            for j in range(BPG):
                grad = value[j * SUB : (j + 1) * SUB]
                rows = pl.ds(first + j, SUB, stride=BPG)
                new = decay_rate * mom[rows, :] + grad
                mom[rows, :] = new
                nest[j, pl.ds(pl.multiple_of(e * SUB, SUB), SUB), :] = grad + decay_rate * new
            return carry

        lax.fori_loop(0, BATCH, one_chunk, 0, unroll=4)
        for half in range(2):
            count_rows = ROW_SPLIT * NCORE * CHUNK
            rows = pl.ds(pl.multiple_of((half * NZ + z) * count_rows, count_rows), count_rows)
            pltpu.make_async_copy(mom.at[rows, :], new_hbm.at[rows, :], local_sems.at[1]).start()
        for j in range(BPG):
            x = nest[j, pl.ds(pl.multiple_of(z * BATCH * SUB, BATCH * SUB), BATCH * SUB), :]
            gram[j] += dot(x, x, left_dim=0)

    def absorb_turn(turn, carry):
        absorb(turn, BATCH)
        return carry

    lax.fori_loop(0, NZ - 1, absorb_turn, 0)
    absorb(NZ - 1, BATCH - 1)

    gram_in[my_k] = gram[my_y]
    for kk in range(1, ROW_SPLIT):
        k = target_k(kk)
        pltpu.make_async_remote_copy(
            src_ref=gram.at[k // 2],
            dst_ref=gram_in.at[my_k],
            send_sem=gram_sems.at[0],
            recv_sem=gram_sems.at[1],
            device_id=(f - my_k + k, o),
            device_id_type=MESH,
        ).start()
    seven = gram_in.at[pl.ds(0, ROW_SPLIT - 1)]
    pltpu.make_async_remote_copy(
        src_ref=seven,
        dst_ref=seven,
        send_sem=gram_sems.at[0],
        recv_sem=gram_sems.at[1],
        device_id=(f, o),
        device_id_type=MESH,
    ).wait()

    now = gram_in[0]
    for k in range(1, ROW_SPLIT):
        now = now + gram_in[k]
    eye = jnp.where(
        lax.broadcasted_iota(jnp.int32, (HD, HD), 0) == lax.broadcasted_iota(jnp.int32, (HD, HD), 1), 1.0, 0.0
    )
    inverse = 1.0 / (jnp.sqrt(jnp.sum(now * eye, axis=(0, 1), keepdims=True)) + epsilon)
    now = now * inverse * inverse
    total = None
    for step in range(ITERS):
        factor = first_coeff * eye + second_coeff * now + third_coeff * dot(now, now)
        total = factor if total is None else dot(total, factor)
        if step < ITERS - 1:
            now = dot(factor, dot(now, factor))
    chain[my_y] = total * (gain_factor * math.sqrt(max(D, HD)) * inverse)
    for dy in range(1, NY):
        y = (my_y + dy) % NY
        pltpu.make_async_remote_copy(
            src_ref=chain.at[my_y],
            dst_ref=chain.at[my_y],
            send_sem=chain_sems.at[0],
            recv_sem=chain_sems.at[1],
            device_id=(f - my_k + y * 2 + my_core, o),
            device_id_type=MESH,
        ).start()
    three = gram_in.at[pl.ds(0, NY - 1)]
    pltpu.make_async_remote_copy(
        src_ref=three,
        dst_ref=three,
        send_sem=chain_sems.at[0],
        recv_sem=chain_sems.at[1],
        device_id=(f, o),
        device_id_type=MESH,
    ).wait()

    def finish(turn, own):
        z = (my_z + z_offset(turn)) % NZ
        parts = []
        for j in range(BPG):
            x = nest[j, pl.ds(pl.multiple_of(z * BATCH * SUB, BATCH * SUB), BATCH * SUB), :]
            parts.append(dot(x, chain[j]).reshape(BATCH, SUB, HD))
        rows = pl.ds(pl.multiple_of(z * BATCH * CHUNK, BATCH * CHUNK), BATCH * CHUNK)
        back[rows, :] = jnp.stack(parts, axis=1).reshape(BATCH * CHUNK, HD).astype(jnp.bfloat16)

        def give(x, k):
            e, to_f, to_o = place(z, x, k)
            pltpu.make_async_remote_copy(
                src_ref=back.at[chunk_of(e), :],
                dst_ref=ret_hbm.at[chunk_of(my_e), :],
                send_sem=back_send_sem,
                recv_sem=back_recv_sem,
                device_id=(to_f, to_o),
                device_id_type=MESH,
            ).start()

        def give_turn(index, carry):
            kk = index // NX
            give((my_x + index % NX) % NX, target_k(kk))
            return carry

        if own:
            pltpu.make_async_copy(
                back.at[chunk_of(my_e), :], ret_hbm.at[chunk_of(my_e), :], local_sems.at[2]
            ).start()
        lax.fori_loop(1 if own else 0, BATCH, give_turn, 0)

    def finish_turn(turn, carry):
        finish(turn, False)
        return carry

    lax.fori_loop(0, NZ - 1, finish_turn, 0)
    finish(NZ - 1, True)

    pltpu.make_async_copy(mom, new_hbm, local_sems.at[1]).wait()
    pltpu.make_async_copy(back.at[chunk_of(my_e), :], ret_hbm.at[chunk_of(my_e), :], local_sems.at[2]).wait()
    waiter(NDEV - 1, send, send_sem, send_sem).wait_send()
    waiter(NDEV - 1, ret_hbm, back_send_sem, back_recv_sem).wait()


def place_kernel(order_ref, ret_ref, out_ref, wide, stage):
    def widen(index, carry):
        rows = pl.ds(pl.multiple_of(index * 128, 128), 128)
        wide[rows, :] = ret_ref[rows, :].astype(jnp.float32)
        return carry

    lax.fori_loop(0, ROWS // 128, widen, 0)

    def column(p, carry):
        block = order_ref[p]
        j, group = block % BPG, block // BPG
        x, z = (group // 16) * 2 + (group // NZ) % 2, group % NZ
        for k in range(ROW_SPLIT):
            e, _, _ = place(z, x, k)
            stage[pl.ds(k, SUB, stride=ROW_SPLIT), :] = wide[pl.ds(pl.multiple_of(e * CHUNK + j * SUB, SUB), SUB), :]
        out_ref[:, pl.ds(pl.multiple_of(p * HD, HD), HD)] = stage[...].astype(jnp.bfloat16)
        return carry

    lax.fori_loop(0, order_ref.shape[0], column, 0, unroll=2)


def per_device(gradient, momentum, head_order):
    blocks = head_order.shape[0]
    positions = jnp.arange(blocks, dtype=jnp.int32)
    source_of = jnp.sum(
        jnp.where(head_order[:, None] == positions[None, :], positions[:, None], 0), axis=0
    )
    vmem, smem, hbm = (pl.BlockSpec(memory_space=m) for m in (pltpu.VMEM, pltpu.SMEM, pl.ANY))
    returned, new = pl.pallas_call(
        kernel,
        out_shape=(
            jax.ShapeDtypeStruct((ROWS, HD), jnp.bfloat16),
            jax.ShapeDtypeStruct((ROWS, HD), jnp.float32),
        ),
        in_specs=[smem, vmem, hbm],
        out_specs=(hbm, hbm),
        scratch_shapes=[
            pltpu.VMEM((ROWS, HD), jnp.float32),
            pltpu.VMEM((ROWS, HD), jnp.bfloat16),
            pltpu.VMEM((ROWS, HD), jnp.bfloat16),
            pltpu.VMEM((BPG, NDEV * SUB, HD), jnp.float32),
            pltpu.VMEM((ROWS, HD), jnp.bfloat16),
            pltpu.VMEM((BPG, SUB * ROW_SPLIT, HD), jnp.float32),
            pltpu.VMEM((BPG, HD, HD), jnp.float32),
            pltpu.VMEM((ROW_SPLIT, HD, HD), jnp.float32),
            pltpu.VMEM((BPG, HD, HD), jnp.float32),
            pltpu.SemaphoreType.DMA,
            pltpu.SemaphoreType.DMA((NZ,)),
            pltpu.SemaphoreType.DMA,
            pltpu.SemaphoreType.DMA,
            pltpu.SemaphoreType.DMA((2,)),
            pltpu.SemaphoreType.DMA((2,)),
            pltpu.SemaphoreType.DMA((3,)),
        ],
        compiler_params=pltpu.CompilerParams(has_side_effects=True, vmem_limit_bytes=56 * 2**20),
    )(source_of, gradient, momentum.reshape(ROWS, HD))
    placed = pl.pallas_call(
        place_kernel,
        out_shape=jax.ShapeDtypeStruct(gradient.shape, jnp.bfloat16),
        in_specs=[smem, vmem],
        out_specs=vmem,
        scratch_shapes=[
            pltpu.VMEM((ROWS, HD), jnp.float32),
            pltpu.VMEM((SUB * ROW_SPLIT, HD), jnp.float32),
        ],
        compiler_params=pltpu.CompilerParams(vmem_limit_bytes=32 * 2**20),
    )(head_order, returned)
    return (placed, new.reshape(momentum.shape))


def solution(mesh):
    in_specs = (P(("fsdp", "opt"), None), P("fsdp", "opt", None, None, None), P())
    out_specs = (P(("fsdp", "opt"), None), P("fsdp", "opt", None, None, None))
    return jax.shard_map(
        per_device, mesh=mesh, in_specs=in_specs, out_specs=out_specs, check_vma=False
    )
```

```python
import math

import jax
import jax.numpy as jnp
from jax import lax
from jax.experimental import pallas as pl
from jax.experimental.pallas import tpu as pltpu
from jax.sharding import PartitionSpec as P

D = 16384
HD = 128
BPG = 4
ROW_SPLIT = 8
ITERS = 5
NX, NY, NZ, NCORE = 4, 4, 8, 2
NDEV = NX * NY * NZ * NCORE
SUB = 8
HALF = BPG // 2
CHUNK = SUB * HALF
BATCH = NX * ROW_SPLIT
ROWS = 2 * NDEV * CHUNK

decay_rate = 0.95
first_coeff = 3.4445
second_coeff = -4.775
third_coeff = 2.0315
epsilon = 1e-07
gain_factor = 0.2

MESH = pl.DeviceIdType.MESH
HIGHEST = lax.Precision.HIGHEST


def dot(left, right, left_dim=1):
    return lax.dot_general(
        left, right, (((left_dim,), (0,)), ((), ())), precision=HIGHEST, preferred_element_type=jnp.float32
    )


def z_offset(turn):
    back = NZ - 1 - turn
    odd = back % 2
    return odd * ((back + 1) // 2) + (1 - odd) * ((NZ - back // 2) % NZ)


def place(z, x, k):
    return (z * NX + x) * ROW_SPLIT + k, ((x % 2) * NZ + z) * ROW_SPLIT + k, x // 2


def chunk_of(index):
    return pl.ds(pl.multiple_of(index * CHUNK, CHUNK), CHUNK)


def kernel(
    source_ref,
    grad_ref,
    mom_hbm,
    ret_hbm,
    new_hbm,
    mom,
    send,
    recv,
    nest,
    back,
    stage,
    gram,
    pair_in,
    ring_in,
    chain,
    send_sem,
    recv_sem,
    back_sems,
    pair_sems,
    ring_sems,
    chain_sems,
    local_sems,
):
    f, o = lax.axis_index("fsdp"), lax.axis_index("opt")
    my_k = f % ROW_SPLIT
    my_z = (f // ROW_SPLIT) % NZ
    my_x = o * 2 + f // (ROW_SPLIT * NZ)
    my_y, my_core = my_k // 2, my_k % 2
    my_e, _, _ = place(my_z, my_x, my_k)

    mom_in = pltpu.make_async_copy(mom_hbm, mom, local_sems.at[0])
    mom_in.start()

    barrier = pltpu.get_barrier_semaphore()

    def greet(index, carry):
        other = (f * 2 + o + index) % NDEV
        pl.semaphore_signal(barrier, inc=1, device_id=(other // 2, other % 2), device_id_type=MESH)
        return carry

    lax.fori_loop(1, NDEV, greet, 0)
    gram[...] = jnp.zeros_like(gram)
    pl.semaphore_wait(barrier, NDEV - 1)

    def target_k(kk):
        return ((my_y + kk // 2) % NY) * 2 + (my_core + kk % 2) % 2

    def remote(src, dst, one, two, to):
        return pltpu.make_async_remote_copy(
            src_ref=src, dst_ref=dst, send_sem=one, recv_sem=two, device_id=to, device_id_type=MESH
        )

    def give(src, dst, one, two, e, to):
        @pl.when(e != my_e)
        def _():
            remote(src, dst, one, two, to).start()

        @pl.when(e == my_e)
        def _():
            pltpu.make_async_copy(src, dst, two).start()

    def send_turns(h, first, last):
        def send_group(index, carry):
            turn, r = index // NX, index % NX
            z, x = (my_z + z_offset(turn)) % NZ, (my_x + r) % NX
            group = (x // 2) * 16 + (x % 2) * NZ + z
            for j in range(HALF):
                column = source_ref[group * BPG + h * HALF + j] * HD
                stage[j] = grad_ref[:, pl.ds(column, HD)].astype(jnp.float32)
            for kk in range(ROW_SPLIT):
                k = target_k(kk)
                e, to_f, to_o = place(z, x, k)
                parts = [stage[j, pl.ds(k, SUB, stride=ROW_SPLIT), :] for j in range(HALF)]
                send[chunk_of(h * NDEV + e), :] = jnp.concatenate(parts, axis=0).astype(jnp.bfloat16)
                src, dst = send.at[chunk_of(h * NDEV + e), :], recv.at[chunk_of(h * NDEV + my_e), :]
                if kk:
                    remote(src, dst, send_sem, recv_sem.at[h, turn], (to_f, to_o)).start()
                else:
                    give(src, dst, send_sem, recv_sem.at[h, turn], e, (to_f, to_o))
            return carry

        lax.fori_loop(first * NX, last * NX, send_group, 0)

    def absorb_turns(h, first, last):
        def absorb(turn, carry):
            whole = recv.at[pl.ds(0, BATCH * CHUNK), :]
            remote(whole, whole, send_sem, recv_sem.at[h, turn], (f, o)).wait_recv()
            z = (my_z + NZ - z_offset(turn)) % NZ

            def one_chunk(index, carry):
                x, k = index // ROW_SPLIT, index % ROW_SPLIT
                e, from_f, from_o = place(z, x, k)
                value = recv[chunk_of(h * NDEV + e), :].astype(jnp.float32)
                start = (from_f * 2 + from_o) * SUB * BPG
                for j in range(HALF):
                    grad = value[j * SUB : (j + 1) * SUB]
                    rows = pl.ds(start + h * HALF + j, SUB, stride=BPG)
                    new = decay_rate * mom[rows, :] + grad
                    mom[rows, :] = new
                    nest[h * HALF + j, pl.ds(pl.multiple_of(e * SUB, SUB), SUB), :] = grad + decay_rate * new
                return carry

            lax.fori_loop(0, BATCH, one_chunk, 0, unroll=4)
            if h:
                for side in range(2):
                    count = ROW_SPLIT * NCORE * SUB * BPG
                    rows = pl.ds(pl.multiple_of((side * NZ + z) * count, count), count)
                    pltpu.make_async_copy(mom.at[rows, :], new_hbm.at[rows, :], local_sems.at[1]).start()
            for j in range(HALF):
                x = nest[h * HALF + j, pl.ds(pl.multiple_of(z * BATCH * SUB, BATCH * SUB), BATCH * SUB), :]
                gram[h * HALF + j] += dot(x, x, left_dim=0)
            return carry

        lax.fori_loop(first, last, absorb, 0)

    sibling = (f + 1 - 2 * my_core, o)

    def pair_copy(h):
        return remote(
            gram.at[h * HALF + 1 - my_core], pair_in.at[h], pair_sems.at[0, h], pair_sems.at[1, h], sibling
        )

    def ring_start(h):
        pair_copy(h).wait()
        ring_in[h * NY + my_y] = gram[h * HALF + my_core] + pair_in[h]
        for dy in range(1, NY):
            piece = ring_in.at[h * NY + my_y]
            to_f = f - my_k + ((my_y + dy) % NY) * 2 + my_core
            remote(piece, piece, ring_sems.at[0, h], ring_sems.at[1, h], (to_f, o)).start()

    def chain_copy(h):
        piece = chain.at[h * HALF + my_core]
        return remote(piece, piece, chain_sems.at[0, h], chain_sems.at[1, h], sibling)

    def factors(h):
        three = ring_in.at[pl.ds(0, NY - 1)]
        remote(three, three, ring_sems.at[0, h], ring_sems.at[1, h], (f, o)).wait()
        now = ring_in[h * NY]
        for y in range(1, NY):
            now = now + ring_in[h * NY + y]
        rows, columns = (lax.broadcasted_iota(jnp.int32, (HD, HD), d) for d in range(2))
        eye = jnp.where(rows == columns, 1.0, 0.0)
        inverse = 1.0 / (jnp.sqrt(jnp.sum(now * eye, axis=(0, 1), keepdims=True)) + epsilon)
        now = now * inverse * inverse
        total = None
        for step in range(ITERS):
            factor = first_coeff * eye + second_coeff * now + third_coeff * dot(now, now)
            total = factor if total is None else dot(total, factor)
            if step < ITERS - 1:
                now = dot(factor, dot(now, factor))
        chain[h * HALF + my_core] = total * (gain_factor * math.sqrt(max(D, HD)) * inverse)
        chain_copy(h).start()

    def finish_turns(h, first, last):
        def finish(turn, carry):
            z = (my_z + z_offset(turn)) % NZ
            parts = []
            for j in range(HALF):
                x = nest[h * HALF + j, pl.ds(pl.multiple_of(z * BATCH * SUB, BATCH * SUB), BATCH * SUB), :]
                parts.append(dot(x, chain[h * HALF + j]).reshape(BATCH, SUB, HD))
            rows = pl.ds(pl.multiple_of((h * NZ + z) * BATCH * CHUNK, BATCH * CHUNK), BATCH * CHUNK)
            back[rows, :] = jnp.stack(parts, axis=1).reshape(BATCH * CHUNK, HD).astype(jnp.bfloat16)

            def give_turn(index, carry):
                x = (my_x + index % NX) % NX
                e, to_f, to_o = place(z, x, target_k(index // NX))
                src, dst = back.at[chunk_of(h * NDEV + e), :], ret_hbm.at[chunk_of(h * NDEV + my_e), :]
                give(src, dst, back_sems.at[0], back_sems.at[1], e, (to_f, to_o))
                return carry

            lax.fori_loop(0, BATCH, give_turn, 0)
            return carry

        lax.fori_loop(first, last, finish, 0)

    send_turns(0, 0, NZ)
    mom_in.wait()
    absorb_turns(0, 0, 6)
    send_turns(1, 0, 2)
    absorb_turns(0, 6, NZ)
    pair_copy(0).start()
    send_turns(1, 2, 3)
    ring_start(0)
    send_turns(1, 3, NZ)
    factors(0)
    absorb_turns(1, 0, 6)
    chain_copy(0).wait()
    finish_turns(0, 0, 2)
    absorb_turns(1, 6, NZ)
    pair_copy(1).start()
    finish_turns(0, 2, 3)
    ring_start(1)
    finish_turns(0, 3, 6)
    factors(1)
    finish_turns(0, 6, NZ)
    chain_copy(1).wait()
    finish_turns(1, 0, NZ)

    pltpu.make_async_copy(mom, new_hbm, local_sems.at[1]).wait()
    sent = send.at[pl.ds(0, 2 * (NDEV - 1) * CHUNK), :]
    remote(sent, sent, send_sem, send_sem, (f, o)).wait_send()
    remote(sent, sent, back_sems.at[0], back_sems.at[0], (f, o)).wait_send()
    remote(ret_hbm, ret_hbm, back_sems.at[0], back_sems.at[1], (f, o)).wait_recv()


LANES = 4


def place_kernel(order_ref, ret_ref, out_ref, wide, stage):
    def widen(index, carry):
        rows = pl.ds(pl.multiple_of(index * 128, 128), 128)
        wide[rows, :] = ret_ref[rows, :].astype(jnp.float32)
        return carry

    lax.fori_loop(0, ROWS // 128, widen, 0, unroll=2)

    def columns(index, carry):
        for lane in range(LANES):
            p = index * LANES + lane
            block = order_ref[p]
            j, group = block % BPG, block // BPG
            x, z = (group // 16) * 2 + (group // NZ) % 2, group % NZ
            first = ((j // HALF) * NDEV + (z * NX + x) * ROW_SPLIT) * CHUNK + (j % HALF) * SUB
            for k in range(ROW_SPLIT):
                rows = pl.ds(pl.multiple_of(first + k * CHUNK, SUB), SUB)
                stage[lane, pl.ds(k, SUB, stride=ROW_SPLIT), :] = wide[rows, :]
        for lane in range(LANES):
            p = index * LANES + lane
            out_ref[:, pl.ds(pl.multiple_of(p * HD, HD), HD)] = stage[lane].astype(jnp.bfloat16)
        return carry

    lax.fori_loop(0, order_ref.shape[0] // LANES, columns, 0)


def per_device(gradient, momentum, head_order):
    blocks = head_order.shape[0]
    positions = jnp.arange(blocks, dtype=jnp.int32)
    source_of = jnp.sum(
        jnp.where(head_order[:, None] == positions[None, :], positions[:, None], 0), axis=0
    )
    vmem, smem, hbm = (pl.BlockSpec(memory_space=m) for m in (pltpu.VMEM, pltpu.SMEM, pl.ANY))
    returned, new = pl.pallas_call(
        kernel,
        out_shape=(
            jax.ShapeDtypeStruct((ROWS, HD), jnp.bfloat16),
            jax.ShapeDtypeStruct((ROWS, HD), jnp.float32),
        ),
        in_specs=[smem, vmem, hbm],
        out_specs=(hbm, hbm),
        scratch_shapes=[
            pltpu.VMEM((ROWS, HD), jnp.float32),
            pltpu.VMEM((ROWS, HD), jnp.bfloat16),
            pltpu.VMEM((ROWS, HD), jnp.bfloat16),
            pltpu.VMEM((BPG, NDEV * SUB, HD), jnp.float32),
            pltpu.VMEM((ROWS, HD), jnp.bfloat16),
            pltpu.VMEM((HALF, SUB * ROW_SPLIT, HD), jnp.float32),
            pltpu.VMEM((BPG, HD, HD), jnp.float32),
            pltpu.VMEM((2, HD, HD), jnp.float32),
            pltpu.VMEM((2 * NY, HD, HD), jnp.float32),
            pltpu.VMEM((BPG, HD, HD), jnp.float32),
            pltpu.SemaphoreType.DMA,
            pltpu.SemaphoreType.DMA((2, NZ)),
            pltpu.SemaphoreType.DMA((2,)),
            pltpu.SemaphoreType.DMA((2, 2)),
            pltpu.SemaphoreType.DMA((2, 2)),
            pltpu.SemaphoreType.DMA((2, 2)),
            pltpu.SemaphoreType.DMA((2,)),
        ],
        compiler_params=pltpu.CompilerParams(
            collective_id=0, has_side_effects=True, vmem_limit_bytes=56 * 2**20
        ),
    )(source_of, gradient, momentum.reshape(ROWS, HD))
    placed = pl.pallas_call(
        place_kernel,
        out_shape=jax.ShapeDtypeStruct(gradient.shape, jnp.bfloat16),
        in_specs=[smem, vmem],
        out_specs=vmem,
        scratch_shapes=[
            pltpu.VMEM((ROWS, HD), jnp.float32),
            pltpu.VMEM((LANES, SUB * ROW_SPLIT, HD), jnp.float32),
        ],
        compiler_params=pltpu.CompilerParams(vmem_limit_bytes=32 * 2**20),
    )(head_order, returned)
    return (placed, new.reshape(momentum.shape))


def solution(mesh):
    in_specs = (P(("fsdp", "opt"), None), P("fsdp", "opt", None, None, None), P())
    out_specs = (P(("fsdp", "opt"), None), P("fsdp", "opt", None, None, None))
    return jax.shard_map(
        per_device, mesh=mesh, in_specs=in_specs, out_specs=out_specs, check_vma=False
    )
```

```python
import math

import jax
import jax.numpy as jnp
from jax import lax
from jax.experimental import pallas as pl
from jax.experimental.pallas import tpu as pltpu
from jax.sharding import PartitionSpec as P

D = 16384
HD = 128
BPG = 4
ROW_SPLIT = 8
ITERS = 5
NX, NY, NZ, NCORE = 4, 4, 8, 2
NDEV = NX * NY * NZ * NCORE
SUB = 8
HALF = BPG // 2
CHUNK = SUB * HALF
BATCH = NX * ROW_SPLIT
ROWS = 2 * NDEV * CHUNK

decay_rate = 0.95
first_coeff = 3.4445
second_coeff = -4.775
third_coeff = 2.0315
epsilon = 1e-07
gain_factor = 0.2

MESH = pl.DeviceIdType.MESH
HIGHEST = lax.Precision.HIGHEST


def dot(left, right, left_dim=1):
    return lax.dot_general(
        left, right, (((left_dim,), (0,)), ((), ())), precision=HIGHEST, preferred_element_type=jnp.float32
    )


def z_offset(turn):
    back = NZ - 1 - turn
    odd = back % 2
    return odd * ((back + 1) // 2) + (1 - odd) * ((NZ - back // 2) % NZ)


def place(z, x, k):
    return (z * NX + x) * ROW_SPLIT + k, ((x % 2) * NZ + z) * ROW_SPLIT + k, x // 2


def chunk_of(index):
    return pl.ds(pl.multiple_of(index * CHUNK, CHUNK), CHUNK)


def kernel(
    source_ref,
    grad_ref,
    mom_hbm,
    ret_hbm,
    new_hbm,
    mom,
    send,
    recv,
    nest,
    back,
    stage,
    gram,
    pair_in,
    ring_in,
    chain,
    send_sem,
    recv_sem,
    back_sems,
    pair_sems,
    ring_sems,
    chain_sems,
    local_sems,
):
    f, o = lax.axis_index("fsdp"), lax.axis_index("opt")
    my_k = f % ROW_SPLIT
    my_z = (f // ROW_SPLIT) % NZ
    my_x = o * 2 + f // (ROW_SPLIT * NZ)
    my_y, my_core = my_k // 2, my_k % 2
    my_e, _, _ = place(my_z, my_x, my_k)

    mom_in = pltpu.make_async_copy(mom_hbm, mom, local_sems.at[0])
    mom_in.start()

    barrier = pltpu.get_barrier_semaphore()

    leader = (my_k == 0) & (o == 0)
    root = leader & (f == 0)
    groups, members = NX * NZ // 2, 2 * ROW_SPLIT

    def signal(to):
        pl.semaphore_signal(barrier, inc=1, device_id=to, device_id_type=MESH)

    @pl.when(jnp.logical_not(leader))
    def _():
        signal((f - my_k, 0))
        pl.semaphore_wait(barrier, 1)

    @pl.when(leader & (f != 0))
    def _():
        pl.semaphore_wait(barrier, members - 1)
        signal((0, 0))
        pl.semaphore_wait(barrier, 1)

    @pl.when(root)
    def _():
        pl.semaphore_wait(barrier, groups + members - 2)

        def to_leader(group, carry):
            signal((group * ROW_SPLIT, 0))
            return carry

        lax.fori_loop(1, groups, to_leader, 0)

    @pl.when(leader)
    def _():
        def to_member(index, carry):
            signal((f + index // 2, index % 2))
            return carry

        lax.fori_loop(1, members, to_member, 0)

    gram[...] = jnp.zeros_like(gram)

    def target_k(kk):
        return ((my_y + kk // 2) % NY) * 2 + (my_core + kk % 2) % 2

    def remote(src, dst, one, two, to):
        return pltpu.make_async_remote_copy(
            src_ref=src, dst_ref=dst, send_sem=one, recv_sem=two, device_id=to, device_id_type=MESH
        )

    def give(src, dst, one, two, e, to):
        @pl.when(e != my_e)
        def _():
            remote(src, dst, one, two, to).start()

        @pl.when(e == my_e)
        def _():
            pltpu.make_async_copy(src, dst, two).start()

    def send_turns(h, first, last):
        def send_group(index, carry):
            turn, r = index // NX, index % NX
            z, x = (my_z + z_offset(turn)) % NZ, (my_x + r) % NX
            group = (x // 2) * 16 + (x % 2) * NZ + z
            for j in range(HALF):
                column = source_ref[group * BPG + h * HALF + j] * HD
                stage[j] = grad_ref[:, pl.ds(column, HD)].astype(jnp.float32)
            for kk in range(ROW_SPLIT):
                k = target_k(kk)
                e, to_f, to_o = place(z, x, k)
                parts = [stage[j, pl.ds(k, SUB, stride=ROW_SPLIT), :] for j in range(HALF)]
                send[chunk_of(h * NDEV + e), :] = jnp.concatenate(parts, axis=0).astype(jnp.bfloat16)
                src, dst = send.at[chunk_of(h * NDEV + e), :], recv.at[chunk_of(h * NDEV + my_e), :]
                if kk:
                    remote(src, dst, send_sem, recv_sem.at[h, turn], (to_f, to_o)).start()
                else:
                    give(src, dst, send_sem, recv_sem.at[h, turn], e, (to_f, to_o))
            return carry

        lax.fori_loop(first * NX, last * NX, send_group, 0)

    def absorb_turns(h, first, last):
        def absorb(turn, carry):
            whole = recv.at[pl.ds(0, BATCH * CHUNK), :]
            remote(whole, whole, send_sem, recv_sem.at[h, turn], (f, o)).wait_recv()
            z = (my_z + NZ - z_offset(turn)) % NZ

            def one_chunk(index, carry):
                x, k = index // ROW_SPLIT, index % ROW_SPLIT
                e, from_f, from_o = place(z, x, k)
                value = recv[chunk_of(h * NDEV + e), :].astype(jnp.float32)
                start = (from_f * 2 + from_o) * SUB * BPG
                for j in range(HALF):
                    grad = value[j * SUB : (j + 1) * SUB]
                    rows = pl.ds(start + h * HALF + j, SUB, stride=BPG)
                    new = decay_rate * mom[rows, :] + grad
                    mom[rows, :] = new
                    nest[h * HALF + j, pl.ds(pl.multiple_of(e * SUB, SUB), SUB), :] = grad + decay_rate * new
                return carry

            lax.fori_loop(0, BATCH, one_chunk, 0, unroll=4)
            if h:
                for side in range(2):
                    count = ROW_SPLIT * NCORE * SUB * BPG
                    rows = pl.ds(pl.multiple_of((side * NZ + z) * count, count), count)
                    pltpu.make_async_copy(mom.at[rows, :], new_hbm.at[rows, :], local_sems.at[1]).start()
            for j in range(HALF):
                x = nest[h * HALF + j, pl.ds(pl.multiple_of(z * BATCH * SUB, BATCH * SUB), BATCH * SUB), :]
                gram[h * HALF + j] += dot(x, x, left_dim=0)
            return carry

        lax.fori_loop(first, last, absorb, 0)

    sibling = (f + 1 - 2 * my_core, o)

    def pair_copy(h):
        return remote(
            gram.at[h * HALF + 1 - my_core], pair_in.at[h], pair_sems.at[0, h], pair_sems.at[1, h], sibling
        )

    def ring_start(h):
        pair_copy(h).wait()
        ring_in[h * NY + my_y] = gram[h * HALF + my_core] + pair_in[h]
        for dy in range(1, NY):
            piece = ring_in.at[h * NY + my_y]
            to_f = f - my_k + ((my_y + dy) % NY) * 2 + my_core
            remote(piece, piece, ring_sems.at[0, h], ring_sems.at[1, h], (to_f, o)).start()

    def chain_copy(h):
        piece = chain.at[h * HALF + my_core]
        return remote(piece, piece, chain_sems.at[0, h], chain_sems.at[1, h], sibling)

    def factors(h):
        three = ring_in.at[pl.ds(0, NY - 1)]
        remote(three, three, ring_sems.at[0, h], ring_sems.at[1, h], (f, o)).wait()
        now = ring_in[h * NY]
        for y in range(1, NY):
            now = now + ring_in[h * NY + y]
        rows, columns = (lax.broadcasted_iota(jnp.int32, (HD, HD), d) for d in range(2))
        eye = jnp.where(rows == columns, 1.0, 0.0)
        inverse = 1.0 / (jnp.sqrt(jnp.sum(now * eye, axis=(0, 1), keepdims=True)) + epsilon)
        now = now * inverse * inverse
        total = None
        for step in range(ITERS):
            factor = first_coeff * eye + second_coeff * now + third_coeff * dot(now, now)
            total = factor if total is None else dot(total, factor)
            if step < ITERS - 1:
                now = dot(factor, dot(now, factor))
        chain[h * HALF + my_core] = total * (gain_factor * math.sqrt(max(D, HD)) * inverse)
        chain_copy(h).start()

    def finish_turns(h, first, last):
        def finish(turn, carry):
            z = (my_z + z_offset(turn)) % NZ
            parts = []
            for j in range(HALF):
                x = nest[h * HALF + j, pl.ds(pl.multiple_of(z * BATCH * SUB, BATCH * SUB), BATCH * SUB), :]
                parts.append(dot(x, chain[h * HALF + j]).reshape(BATCH, SUB, HD))
            rows = pl.ds(pl.multiple_of((h * NZ + z) * BATCH * CHUNK, BATCH * CHUNK), BATCH * CHUNK)
            back[rows, :] = jnp.stack(parts, axis=1).reshape(BATCH * CHUNK, HD).astype(jnp.bfloat16)

            def give_turn(index, carry):
                x = (my_x + index % NX) % NX
                e, to_f, to_o = place(z, x, target_k(index // NX))
                src, dst = back.at[chunk_of(h * NDEV + e), :], ret_hbm.at[chunk_of(h * NDEV + my_e), :]
                give(src, dst, back_sems.at[0], back_sems.at[1], e, (to_f, to_o))
                return carry

            lax.fori_loop(0, BATCH, give_turn, 0)
            return carry

        lax.fori_loop(first, last, finish, 0)

    send_turns(0, 0, NZ)
    mom_in.wait()
    absorb_turns(0, 0, 6)
    send_turns(1, 0, 2)
    absorb_turns(0, 6, NZ)
    pair_copy(0).start()
    send_turns(1, 2, 3)
    ring_start(0)
    send_turns(1, 3, NZ)
    factors(0)
    absorb_turns(1, 0, 6)
    chain_copy(0).wait()
    finish_turns(0, 0, 2)
    absorb_turns(1, 6, NZ)
    pair_copy(1).start()
    finish_turns(0, 2, 3)
    ring_start(1)
    finish_turns(0, 3, 6)
    factors(1)
    finish_turns(0, 6, NZ)
    chain_copy(1).wait()
    finish_turns(1, 0, NZ)

    pltpu.make_async_copy(mom, new_hbm, local_sems.at[1]).wait()
    sent = send.at[pl.ds(0, 2 * (NDEV - 1) * CHUNK), :]
    remote(sent, sent, send_sem, send_sem, (f, o)).wait_send()
    remote(sent, sent, back_sems.at[0], back_sems.at[0], (f, o)).wait_send()
    remote(ret_hbm, ret_hbm, back_sems.at[0], back_sems.at[1], (f, o)).wait_recv()


PIECES = 8


def place_kernel(order_ref, ret_hbm, new_hbm, out_hbm, kept_hbm, ret, wide, out, kept, in_sems, out_sems):
    rows_of = [pl.ds(i * (ROWS // PIECES), ROWS // PIECES) for i in range(PIECES)]
    for i, rows in enumerate(rows_of):
        pltpu.make_async_copy(ret_hbm.at[rows, :], ret.at[rows, :], in_sems.at[i]).start()
    for rows in rows_of:
        pltpu.make_async_copy(new_hbm.at[rows, :], kept.at[rows, :], out_sems.at[0]).start()

    for i, rows in enumerate(rows_of):
        pltpu.make_async_copy(ret_hbm.at[rows, :], ret.at[rows, :], in_sems.at[i]).wait()

        def widen(index, carry):
            some = pl.ds(pl.multiple_of(i * (ROWS // PIECES) + index * 128, 128), 128)
            wide[some, :] = ret[some, :].astype(jnp.float32)
            return carry

        lax.fori_loop(0, ROWS // PIECES // 128, widen, 0, unroll=2)

    pltpu.make_async_copy(new_hbm, kept, out_sems.at[0]).wait()
    for rows in rows_of:
        pltpu.make_async_copy(kept.at[rows, :], kept_hbm.at[rows, :], out_sems.at[1]).start()

    columns = order_ref.shape[0] // PIECES
    for i in range(PIECES):

        def column(index, carry):
            p = i * columns + index
            block = order_ref[p]
            j, group = block % BPG, block // BPG
            x, z = (group // 16) * 2 + (group // NZ) % 2, group % NZ
            first = ((j // HALF) * NDEV + (z * NX + x) * ROW_SPLIT) * CHUNK + (j % HALF) * SUB
            tiles = [wide[pl.ds(first + row, ROW_SPLIT, stride=CHUNK), :] for row in range(SUB)]
            out[:, pl.ds(pl.multiple_of(p * HD, HD), HD)] = jnp.concatenate(tiles, axis=0).astype(jnp.bfloat16)
            return carry

        lax.fori_loop(0, columns, column, 0, unroll=4)
        panel = pl.ds(i * columns * HD, columns * HD)
        pltpu.make_async_copy(out.at[:, panel], out_hbm.at[:, panel], out_sems.at[2]).start()

    pltpu.make_async_copy(kept, kept_hbm, out_sems.at[1]).wait()
    pltpu.make_async_copy(out, out_hbm, out_sems.at[2]).wait()


def per_device(gradient, momentum, head_order):
    blocks = head_order.shape[0]
    positions = jnp.arange(blocks, dtype=jnp.int32)
    source_of = jnp.sum(
        jnp.where(head_order[:, None] == positions[None, :], positions[:, None], 0), axis=0
    )
    vmem, smem, hbm = (pl.BlockSpec(memory_space=m) for m in (pltpu.VMEM, pltpu.SMEM, pl.ANY))
    returned, new = pl.pallas_call(
        kernel,
        out_shape=(
            jax.ShapeDtypeStruct((ROWS, HD), jnp.bfloat16),
            jax.ShapeDtypeStruct((ROWS, HD), jnp.float32),
        ),
        in_specs=[smem, vmem, hbm],
        out_specs=(hbm, hbm),
        scratch_shapes=[
            pltpu.VMEM((ROWS, HD), jnp.float32),
            pltpu.VMEM((ROWS, HD), jnp.bfloat16),
            pltpu.VMEM((ROWS, HD), jnp.bfloat16),
            pltpu.VMEM((BPG, NDEV * SUB, HD), jnp.float32),
            pltpu.VMEM((ROWS, HD), jnp.bfloat16),
            pltpu.VMEM((HALF, SUB * ROW_SPLIT, HD), jnp.float32),
            pltpu.VMEM((BPG, HD, HD), jnp.float32),
            pltpu.VMEM((2, HD, HD), jnp.float32),
            pltpu.VMEM((2 * NY, HD, HD), jnp.float32),
            pltpu.VMEM((BPG, HD, HD), jnp.float32),
            pltpu.SemaphoreType.DMA,
            pltpu.SemaphoreType.DMA((2, NZ)),
            pltpu.SemaphoreType.DMA((2,)),
            pltpu.SemaphoreType.DMA((2, 2)),
            pltpu.SemaphoreType.DMA((2, 2)),
            pltpu.SemaphoreType.DMA((2, 2)),
            pltpu.SemaphoreType.DMA((2,)),
        ],
        compiler_params=pltpu.CompilerParams(
            collective_id=0, has_side_effects=True, vmem_limit_bytes=56 * 2**20
        ),
    )(source_of, gradient, momentum.reshape(ROWS, HD))
    placed, kept = pl.pallas_call(
        place_kernel,
        out_shape=(
            jax.ShapeDtypeStruct(gradient.shape, jnp.bfloat16),
            jax.ShapeDtypeStruct((ROWS, HD), jnp.float32),
        ),
        in_specs=[smem, hbm, hbm],
        out_specs=(hbm, hbm),
        scratch_shapes=[
            pltpu.VMEM((ROWS, HD), jnp.bfloat16),
            pltpu.VMEM((ROWS, HD), jnp.float32),
            pltpu.VMEM(gradient.shape, jnp.bfloat16),
            pltpu.VMEM((ROWS, HD), jnp.float32),
            pltpu.SemaphoreType.DMA((PIECES,)),
            pltpu.SemaphoreType.DMA((3,)),
        ],
        compiler_params=pltpu.CompilerParams(vmem_limit_bytes=58 * 2**20),
    )(head_order, returned, new)
    return (placed, kept.reshape(momentum.shape))


def solution(mesh):
    in_specs = (P(("fsdp", "opt"), None), P("fsdp", "opt", None, None, None), P())
    out_specs = (P(("fsdp", "opt"), None), P("fsdp", "opt", None, None, None))
    return jax.shard_map(
        per_device, mesh=mesh, in_specs=in_specs, out_specs=out_specs, check_vma=False
    )
```

```python
import math

import jax
import jax.numpy as jnp
from jax import lax
from jax.experimental import pallas as pl
from jax.experimental.pallas import tpu as pltpu
from jax.sharding import PartitionSpec as P

D = 16384
HD = 128
BPG = 4
ROW_SPLIT = 8
ITERS = 5
NX, NY, NZ, NCORE = 4, 4, 8, 2
NDEV = NX * NY * NZ * NCORE
SUB = 8
HALF = BPG // 2
CHUNK = SUB * HALF
BATCH = NX * ROW_SPLIT
ROWS = 2 * NDEV * CHUNK

decay_rate = 0.95
first_coeff = 3.4445
second_coeff = -4.775
third_coeff = 2.0315
epsilon = 1e-07
gain_factor = 0.2

MESH = pl.DeviceIdType.MESH
HIGHEST = lax.Precision.HIGHEST


def dot(left, right, left_dim=1):
    return lax.dot_general(
        left, right, (((left_dim,), (0,)), ((), ())), precision=HIGHEST, preferred_element_type=jnp.float32
    )


def split(value):
    high = value.astype(jnp.bfloat16)
    return high, (value - high.astype(jnp.float32)).astype(jnp.bfloat16)


def dot_split(left, right):
    (a, b), (c, d) = split(left), split(right)
    return sum(jnp.dot(u, v, preferred_element_type=jnp.float32) for u, v in ((b, c), (a, d), (a, c)))


def z_offset(turn):
    back = NZ - 1 - turn
    odd = back % 2
    return odd * ((back + 1) // 2) + (1 - odd) * ((NZ - back // 2) % NZ)


def place(z, x, k):
    return (z * NX + x) * ROW_SPLIT + k, ((x % 2) * NZ + z) * ROW_SPLIT + k, x // 2


def chunk_of(index):
    return pl.ds(pl.multiple_of(index * CHUNK, CHUNK), CHUNK)


def kernel(
    source_ref,
    grad_hbm,
    mom_hbm,
    ret_hbm,
    new_hbm,
    grad_ref,
    mom,
    send,
    recv,
    nest,
    back,
    stage,
    gram,
    pair_in,
    ring_in,
    chain,
    send_sem,
    recv_sem,
    back_sems,
    pair_sems,
    ring_sems,
    chain_sems,
    local_sems,
):
    f, o = lax.axis_index("fsdp"), lax.axis_index("opt")
    my_k = f % ROW_SPLIT
    my_z = (f // ROW_SPLIT) % NZ
    my_x = o * 2 + f // (ROW_SPLIT * NZ)
    my_y, my_core = my_k // 2, my_k % 2
    my_e, _, _ = place(my_z, my_x, my_k)

    mom_in = pltpu.make_async_copy(mom_hbm, mom, local_sems.at[0])
    grad_in = pltpu.make_async_copy(grad_hbm, grad_ref, local_sems.at[2])
    grad_in.start()
    mom_in.start()

    barrier = pltpu.get_barrier_semaphore()

    leader = (my_k == 0) & (o == 0)
    root = leader & (f == 0)
    groups, members = NX * NZ // 2, 2 * ROW_SPLIT

    def signal(to):
        pl.semaphore_signal(barrier, inc=1, device_id=to, device_id_type=MESH)

    @pl.when(jnp.logical_not(leader))
    def _():
        signal((f - my_k, 0))
        pl.semaphore_wait(barrier, 1)

    @pl.when(leader & (f != 0))
    def _():
        pl.semaphore_wait(barrier, members - 1)
        signal((0, 0))
        pl.semaphore_wait(barrier, 1)

    @pl.when(root)
    def _():
        pl.semaphore_wait(barrier, groups + members - 2)

        def to_leader(group, carry):
            signal((group * ROW_SPLIT, 0))
            return carry

        lax.fori_loop(1, groups, to_leader, 0)

    @pl.when(leader)
    def _():
        def to_member(index, carry):
            signal((f + index // 2, index % 2))
            return carry

        lax.fori_loop(1, members, to_member, 0)

    gram[...] = jnp.zeros_like(gram)

    target_k = [((my_y + kk // 2) % NY) * 2 + (my_core + kk % 2) % 2 for kk in range(ROW_SPLIT)]

    def remote(src, dst, one, two, to):
        return pltpu.make_async_remote_copy(
            src_ref=src, dst_ref=dst, send_sem=one, recv_sem=two, device_id=to, device_id_type=MESH
        )

    def give(src, dst, one, two, e, to):
        @pl.when(e != my_e)
        def _():
            remote(src, dst, one, two, to).start()

        @pl.when(e == my_e)
        def _():
            pltpu.make_async_copy(src, dst, two).start()

    def send_turns(h, first, last):
        def send_group(index, carry):
            turn, r = index // NX, index % NX
            z, x = (my_z + z_offset(turn)) % NZ, (my_x + r) % NX
            group = (x // 2) * 16 + (x % 2) * NZ + z
            for j in range(HALF):
                column = source_ref[group * BPG + h * HALF + j] * HD
                stage[j] = grad_ref[:, pl.ds(column, HD)].astype(jnp.float32)
            for kk in range(ROW_SPLIT):
                k = target_k[kk]
                e, to_f, to_o = place(z, x, k)
                parts = [stage[j, pl.ds(k, SUB, stride=ROW_SPLIT), :] for j in range(HALF)]
                send[chunk_of(h * NDEV + e), :] = jnp.concatenate(parts, axis=0).astype(jnp.bfloat16)
                src, dst = send.at[chunk_of(h * NDEV + e), :], recv.at[chunk_of(h * NDEV + my_e), :]
                if kk:
                    remote(src, dst, send_sem, recv_sem.at[h, turn], (to_f, to_o)).start()
                else:
                    give(src, dst, send_sem, recv_sem.at[h, turn], e, (to_f, to_o))
            return carry

        lax.fori_loop(first * NX, last * NX, send_group, 0)

    def absorb_turns(h, first, last):
        def absorb(turn, carry):
            whole = recv.at[pl.ds(0, BATCH * CHUNK), :]
            remote(whole, whole, send_sem, recv_sem.at[h, turn], (f, o)).wait_recv()
            z = (my_z + NZ - z_offset(turn)) % NZ

            def one_chunk(index, carry):
                x, k = index // ROW_SPLIT, index % ROW_SPLIT
                e, from_f, from_o = place(z, x, k)
                value = recv[chunk_of(h * NDEV + e), :].astype(jnp.float32)
                start = (from_f * 2 + from_o) * SUB * BPG
                for j in range(HALF):
                    grad = value[j * SUB : (j + 1) * SUB]
                    rows = pl.ds(start + h * HALF + j, SUB, stride=BPG)
                    new = decay_rate * mom[rows, :] + grad
                    mom[rows, :] = new
                    nest[h * HALF + j, pl.ds(pl.multiple_of(e * SUB, SUB), SUB), :] = grad + decay_rate * new
                return carry

            lax.fori_loop(0, BATCH, one_chunk, 0, unroll=4)
            if h:
                for side in range(2):
                    count = ROW_SPLIT * NCORE * SUB * BPG
                    rows = pl.ds(pl.multiple_of((side * NZ + z) * count, count), count)
                    pltpu.make_async_copy(mom.at[rows, :], new_hbm.at[rows, :], local_sems.at[1]).start()
            for j in range(HALF):
                x = nest[h * HALF + j, pl.ds(pl.multiple_of(z * BATCH * SUB, BATCH * SUB), BATCH * SUB), :]
                gram[h * HALF + j] += dot(x, x, left_dim=0)
            return carry

        lax.fori_loop(first, last, absorb, 0)

    sibling = (f + 1 - 2 * my_core, o)

    def pair_copy(h):
        return remote(
            gram.at[h * HALF + 1 - my_core], pair_in.at[h], pair_sems.at[0, h], pair_sems.at[1, h], sibling
        )

    def ring_start(h):
        pair_copy(h).wait()
        ring_in[h * NY + my_y] = gram[h * HALF + my_core] + pair_in[h]
        for dy in range(1, NY):
            piece = ring_in.at[h * NY + my_y]
            to_f = f - my_k + ((my_y + dy) % NY) * 2 + my_core
            remote(piece, piece, ring_sems.at[0, h], ring_sems.at[1, h], (to_f, o)).start()

    def chain_copy(h):
        piece = chain.at[h * HALF + my_core]
        return remote(piece, piece, chain_sems.at[0, h], chain_sems.at[1, h], sibling)

    def factors(h):
        three = ring_in.at[pl.ds(0, NY - 1)]
        remote(three, three, ring_sems.at[0, h], ring_sems.at[1, h], (f, o)).wait()
        now = ring_in[h * NY]
        for y in range(1, NY):
            now = now + ring_in[h * NY + y]
        rows, columns = (lax.broadcasted_iota(jnp.int32, (HD, HD), d) for d in range(2))
        eye = jnp.where(rows == columns, 1.0, 0.0)
        inverse = 1.0 / (jnp.sqrt(jnp.sum(now * eye, axis=(0, 1), keepdims=True)) + epsilon)
        now = now * inverse * inverse
        total = None
        for step in range(ITERS):
            factor = first_coeff * eye + second_coeff * now + third_coeff * dot(now, now)
            total = factor if total is None else dot(total, factor)
            if step < ITERS - 1:
                now = dot(factor, dot(now, factor))
        chain[h * HALF + my_core] = total * (gain_factor * math.sqrt(max(D, HD)) * inverse)
        chain_copy(h).start()

    def finish_turns(h, first, last):
        def finish(turn, carry):
            z = (my_z + z_offset(turn)) % NZ
            parts = []
            for j in range(HALF):
                x = nest[h * HALF + j, pl.ds(pl.multiple_of(z * BATCH * SUB, BATCH * SUB), BATCH * SUB), :]
                parts.append(dot_split(x, chain[h * HALF + j]).reshape(BATCH, SUB, HD))
            rows = pl.ds(pl.multiple_of((h * NZ + z) * BATCH * CHUNK, BATCH * CHUNK), BATCH * CHUNK)
            back[rows, :] = jnp.stack(parts, axis=1).reshape(BATCH * CHUNK, HD).astype(jnp.bfloat16)

            def give_row(r, carry):
                x = (my_x + r) % NX
                for kk in range(ROW_SPLIT):
                    e, to_f, to_o = place(z, x, target_k[kk])
                    src, dst = back.at[chunk_of(h * NDEV + e), :], ret_hbm.at[chunk_of(h * NDEV + my_e), :]
                    if kk:
                        remote(src, dst, back_sems.at[0], back_sems.at[1], (to_f, to_o)).start()
                    else:
                        give(src, dst, back_sems.at[0], back_sems.at[1], e, (to_f, to_o))
                return carry

            lax.fori_loop(0, NX, give_row, 0)
            return carry

        lax.fori_loop(first, last, finish, 0)

    grad_in.wait()
    send_turns(0, 0, NZ)
    send_turns(1, 0, 4)
    mom_in.wait()
    absorb_turns(0, 0, NZ)
    pair_copy(0).start()
    send_turns(1, 4, 5)
    ring_start(0)
    send_turns(1, 5, NZ)
    factors(0)
    chain_copy(0).wait()
    finish_turns(0, 0, 4)
    absorb_turns(1, 0, NZ)
    pair_copy(1).start()
    finish_turns(0, 4, 5)
    ring_start(1)
    finish_turns(0, 5, 8)
    factors(1)
    chain_copy(1).wait()
    finish_turns(1, 0, NZ)

    pltpu.make_async_copy(mom, new_hbm, local_sems.at[1]).wait()
    sent = send.at[pl.ds(0, 2 * (NDEV - 1) * CHUNK), :]
    remote(sent, sent, send_sem, send_sem, (f, o)).wait_send()
    remote(sent, sent, back_sems.at[0], back_sems.at[0], (f, o)).wait_send()
    remote(ret_hbm, ret_hbm, back_sems.at[0], back_sems.at[1], (f, o)).wait_recv()


PIECES = 8


def place_kernel(order_ref, ret_hbm, new_hbm, out_hbm, kept_hbm, ret, wide, out, kept, in_sems, out_sems):
    rows_of = [pl.ds(i * (ROWS // PIECES), ROWS // PIECES) for i in range(PIECES)]
    for i, rows in enumerate(rows_of):
        pltpu.make_async_copy(ret_hbm.at[rows, :], ret.at[rows, :], in_sems.at[i]).start()
    for rows in rows_of:
        pltpu.make_async_copy(new_hbm.at[rows, :], kept.at[rows, :], out_sems.at[0]).start()

    for i, rows in enumerate(rows_of):
        pltpu.make_async_copy(ret_hbm.at[rows, :], ret.at[rows, :], in_sems.at[i]).wait()

        def widen(index, carry):
            some = pl.ds(pl.multiple_of(i * (ROWS // PIECES) + index * 128, 128), 128)
            wide[some, :] = ret[some, :].astype(jnp.float32)
            return carry

        lax.fori_loop(0, ROWS // PIECES // 128, widen, 0, unroll=2)

    columns = order_ref.shape[0] // PIECES
    for i in range(PIECES):

        def column(index, carry):
            p = i * columns + index
            block = order_ref[p]
            j, group = block % BPG, block // BPG
            x, z = (group // 16) * 2 + (group // NZ) % 2, group % NZ
            first = ((j // HALF) * NDEV + (z * NX + x) * ROW_SPLIT) * CHUNK + (j % HALF) * SUB
            tiles = [wide[pl.ds(first + row, ROW_SPLIT, stride=CHUNK), :] for row in range(SUB)]
            out[:, pl.ds(pl.multiple_of(p * HD, HD), HD)] = jnp.concatenate(tiles, axis=0).astype(jnp.bfloat16)
            return carry

        lax.fori_loop(0, columns, column, 0, unroll=8)
        panel = pl.ds(i * columns * HD, columns * HD)
        pltpu.make_async_copy(out.at[:, panel], out_hbm.at[:, panel], out_sems.at[2]).start()
        if i == 0:
            pltpu.make_async_copy(new_hbm, kept, out_sems.at[0]).wait()
            for rows in rows_of:
                pltpu.make_async_copy(kept.at[rows, :], kept_hbm.at[rows, :], out_sems.at[1]).start()

    pltpu.make_async_copy(kept, kept_hbm, out_sems.at[1]).wait()
    pltpu.make_async_copy(out, out_hbm, out_sems.at[2]).wait()


def per_device(gradient, momentum, head_order):
    blocks = head_order.shape[0]
    positions = jnp.arange(blocks, dtype=jnp.int32)
    source_of = jnp.sum(
        jnp.where(head_order[:, None] == positions[None, :], positions[:, None], 0), axis=0
    )
    smem, hbm = (pl.BlockSpec(memory_space=m) for m in (pltpu.SMEM, pl.ANY))
    returned, new = pl.pallas_call(
        kernel,
        out_shape=(
            jax.ShapeDtypeStruct((ROWS, HD), jnp.bfloat16),
            jax.ShapeDtypeStruct((ROWS, HD), jnp.float32),
        ),
        in_specs=[smem, hbm, hbm],
        out_specs=(hbm, hbm),
        scratch_shapes=[
            pltpu.VMEM(gradient.shape, jnp.bfloat16),
            pltpu.VMEM((ROWS, HD), jnp.float32),
            pltpu.VMEM((ROWS, HD), jnp.bfloat16),
            pltpu.VMEM((ROWS, HD), jnp.bfloat16),
            pltpu.VMEM((BPG, NDEV * SUB, HD), jnp.float32),
            pltpu.VMEM((ROWS, HD), jnp.bfloat16),
            pltpu.VMEM((HALF, SUB * ROW_SPLIT, HD), jnp.float32),
            pltpu.VMEM((BPG, HD, HD), jnp.float32),
            pltpu.VMEM((2, HD, HD), jnp.float32),
            pltpu.VMEM((2 * NY, HD, HD), jnp.float32),
            pltpu.VMEM((BPG, HD, HD), jnp.float32),
            pltpu.SemaphoreType.DMA,
            pltpu.SemaphoreType.DMA((2, NZ)),
            pltpu.SemaphoreType.DMA((2,)),
            pltpu.SemaphoreType.DMA((2, 2)),
            pltpu.SemaphoreType.DMA((2, 2)),
            pltpu.SemaphoreType.DMA((2, 2)),
            pltpu.SemaphoreType.DMA((3,)),
        ],
        compiler_params=pltpu.CompilerParams(
            collective_id=0, has_side_effects=True, vmem_limit_bytes=56 * 2**20
        ),
    )(source_of, gradient, momentum.reshape(ROWS, HD))
    placed, kept = pl.pallas_call(
        place_kernel,
        out_shape=(
            jax.ShapeDtypeStruct(gradient.shape, jnp.bfloat16),
            jax.ShapeDtypeStruct((ROWS, HD), jnp.float32),
        ),
        in_specs=[smem, hbm, hbm],
        out_specs=(hbm, hbm),
        scratch_shapes=[
            pltpu.VMEM((ROWS, HD), jnp.bfloat16),
            pltpu.VMEM((ROWS, HD), jnp.float32),
            pltpu.VMEM(gradient.shape, jnp.bfloat16),
            pltpu.VMEM((ROWS, HD), jnp.float32),
            pltpu.SemaphoreType.DMA((PIECES,)),
            pltpu.SemaphoreType.DMA((3,)),
        ],
        compiler_params=pltpu.CompilerParams(vmem_limit_bytes=58 * 2**20),
    )(head_order, returned, new)
    return (placed, kept.reshape(momentum.shape))


def solution(mesh):
    in_specs = (P(("fsdp", "opt"), None), P("fsdp", "opt", None, None, None), P())
    out_specs = (P(("fsdp", "opt"), None), P("fsdp", "opt", None, None, None))
    return jax.shard_map(
        per_device, mesh=mesh, in_specs=in_specs, out_specs=out_specs, check_vma=False
    )
```

```python
import math

import jax
import jax.numpy as jnp
from jax import lax
from jax.experimental import pallas as pl
from jax.experimental.pallas import tpu as pltpu
from jax.sharding import PartitionSpec as P

D = 16384
HD = 128
BPG = 4
ROW_SPLIT = 8
ITERS = 5
NX, NY, NZ, NCORE = 4, 4, 8, 2
NDEV = NX * NY * NZ * NCORE
SUB = 8
HALF = BPG // 2
CHUNK = SUB * HALF
BATCH = NX * ROW_SPLIT
ROWS = 2 * NDEV * CHUNK

decay_rate = 0.95
first_coeff = 3.4445
second_coeff = -4.775
third_coeff = 2.0315
epsilon = 1e-07
gain_factor = 0.2

MESH = pl.DeviceIdType.MESH
HIGHEST = lax.Precision.HIGHEST


def dot(left, right, left_dim=1):
    return lax.dot_general(
        left, right, (((left_dim,), (0,)), ((), ())), precision=HIGHEST, preferred_element_type=jnp.float32
    )


def split(value):
    high = value.astype(jnp.bfloat16)
    return high, (value - high.astype(jnp.float32)).astype(jnp.bfloat16)


def dot_split(left, right):
    (a, b), (c, d) = split(left), split(right)
    return sum(jnp.dot(u, v, preferred_element_type=jnp.float32) for u, v in ((b, c), (a, d), (a, c)))


def z_offset(turn):
    back = NZ - 1 - turn
    odd = back % 2
    return odd * ((back + 1) // 2) + (1 - odd) * ((NZ - back // 2) % NZ)


def place(z, x, k):
    return (z * NX + x) * ROW_SPLIT + k, ((x % 2) * NZ + z) * ROW_SPLIT + k, x // 2


def chunk_of(index):
    return pl.ds(pl.multiple_of(index * CHUNK, CHUNK), CHUNK)


def kernel(
    order_ref,
    grad_hbm,
    mom_hbm,
    ret_hbm,
    new_hbm,
    source_row,
    source_ref,
    grad_ref,
    mom,
    send,
    recv,
    nest,
    back,
    stage,
    gram,
    pair_in,
    ring_in,
    chain,
    send_sem,
    recv_sem,
    back_sems,
    pair_sems,
    ring_sems,
    chain_sems,
    local_sems,
):
    f, o = lax.axis_index("fsdp"), lax.axis_index("opt")
    my_k = f % ROW_SPLIT
    my_z = (f // ROW_SPLIT) % NZ
    my_x = o * 2 + f // (ROW_SPLIT * NZ)
    my_y, my_core = my_k // 2, my_k % 2
    my_e, _, _ = place(my_z, my_x, my_k)

    mom_in = pltpu.make_async_copy(mom_hbm, mom, local_sems.at[0])
    grad_in = pltpu.make_async_copy(grad_hbm, grad_ref, local_sems.at[2])
    grad_in.start()
    mom_in.start()

    down, along = (lax.broadcasted_iota(jnp.int32, (HD, HD), d) for d in range(2))
    held = jnp.broadcast_to(order_ref[...], (HD, HD)).T
    source_row[...] = jnp.max(jnp.where(held == along, down, 0), axis=0, keepdims=True)
    source_in = pltpu.make_async_copy(source_row, source_ref, local_sems.at[3])
    source_in.start()

    barrier = pltpu.get_barrier_semaphore()

    leader = (my_k == 0) & (o == 0)
    root = leader & (f == 0)
    groups, members = NX * NZ // 2, 2 * ROW_SPLIT

    def signal(to):
        pl.semaphore_signal(barrier, inc=1, device_id=to, device_id_type=MESH)

    @pl.when(jnp.logical_not(leader))
    def _():
        signal((f - my_k, 0))
        pl.semaphore_wait(barrier, 1)

    @pl.when(leader & (f != 0))
    def _():
        pl.semaphore_wait(barrier, members - 1)
        signal((0, 0))
        pl.semaphore_wait(barrier, 1)

    @pl.when(root)
    def _():
        pl.semaphore_wait(barrier, groups + members - 2)

        def to_leader(group, carry):
            signal((group * ROW_SPLIT, 0))
            return carry

        lax.fori_loop(1, groups, to_leader, 0)

    @pl.when(leader)
    def _():
        def to_member(index, carry):
            signal((f + index // 2, index % 2))
            return carry

        lax.fori_loop(1, members, to_member, 0)

    gram[...] = jnp.zeros_like(gram)

    target_k = [((my_y + kk // 2) % NY) * 2 + (my_core + kk % 2) % 2 for kk in range(ROW_SPLIT)]

    def remote(src, dst, one, two, to):
        return pltpu.make_async_remote_copy(
            src_ref=src, dst_ref=dst, send_sem=one, recv_sem=two, device_id=to, device_id_type=MESH
        )

    def give(src, dst, one, two, e, to):
        @pl.when(e != my_e)
        def _():
            remote(src, dst, one, two, to).start()

        @pl.when(e == my_e)
        def _():
            pltpu.make_async_copy(src, dst, two).start()

    def send_turns(h, first, last):
        def send_group(index, carry):
            turn, r = index // NX, index % NX
            z, x = (my_z + z_offset(turn)) % NZ, (my_x + r) % NX
            group = (x // 2) * 16 + (x % 2) * NZ + z
            for j in range(HALF):
                column = source_ref[0, group * BPG + h * HALF + j] * HD
                stage[j] = grad_ref[:, pl.ds(column, HD)].astype(jnp.float32)
            for kk in range(ROW_SPLIT):
                k = target_k[kk]
                e, to_f, to_o = place(z, x, k)
                parts = [stage[j, pl.ds(k, SUB, stride=ROW_SPLIT), :] for j in range(HALF)]
                send[chunk_of(h * NDEV + e), :] = jnp.concatenate(parts, axis=0).astype(jnp.bfloat16)
                src, dst = send.at[chunk_of(h * NDEV + e), :], recv.at[chunk_of(h * NDEV + my_e), :]
                if kk:
                    remote(src, dst, send_sem, recv_sem.at[h, turn], (to_f, to_o)).start()
                else:
                    give(src, dst, send_sem, recv_sem.at[h, turn], e, (to_f, to_o))
            return carry

        lax.fori_loop(first * NX, last * NX, send_group, 0)

    def absorb_turns(h, first, last):
        def absorb(turn, carry):
            whole = recv.at[pl.ds(0, BATCH * CHUNK), :]
            remote(whole, whole, send_sem, recv_sem.at[h, turn], (f, o)).wait_recv()
            z = (my_z + NZ - z_offset(turn)) % NZ

            def one_chunk(index, carry):
                x, k = index // ROW_SPLIT, index % ROW_SPLIT
                e, from_f, from_o = place(z, x, k)
                value = recv[chunk_of(h * NDEV + e), :].astype(jnp.float32)
                start = (from_f * 2 + from_o) * SUB * BPG
                for j in range(HALF):
                    grad = value[j * SUB : (j + 1) * SUB]
                    rows = pl.ds(start + h * HALF + j, SUB, stride=BPG)
                    new = decay_rate * mom[rows, :] + grad
                    mom[rows, :] = new
                    nest[h * HALF + j, pl.ds(pl.multiple_of(e * SUB, SUB), SUB), :] = grad + decay_rate * new
                return carry

            lax.fori_loop(0, BATCH, one_chunk, 0, unroll=4)
            if h:
                for side in range(2):
                    count = ROW_SPLIT * NCORE * SUB * BPG
                    rows = pl.ds(pl.multiple_of((side * NZ + z) * count, count), count)
                    pltpu.make_async_copy(mom.at[rows, :], new_hbm.at[rows, :], local_sems.at[1]).start()
            for j in range(HALF):
                x = nest[h * HALF + j, pl.ds(pl.multiple_of(z * BATCH * SUB, BATCH * SUB), BATCH * SUB), :]
                gram[h * HALF + j] += dot(x, x, left_dim=0)
            return carry

        lax.fori_loop(first, last, absorb, 0)

    sibling = (f + 1 - 2 * my_core, o)

    def pair_copy(h):
        return remote(
            gram.at[h * HALF + 1 - my_core], pair_in.at[h], pair_sems.at[0, h], pair_sems.at[1, h], sibling
        )

    def ring_start(h):
        pair_copy(h).wait()
        ring_in[h * NY + my_y] = gram[h * HALF + my_core] + pair_in[h]
        for dy in range(1, NY):
            piece = ring_in.at[h * NY + my_y]
            to_f = f - my_k + ((my_y + dy) % NY) * 2 + my_core
            remote(piece, piece, ring_sems.at[0, h], ring_sems.at[1, h], (to_f, o)).start()

    def chain_copy(h):
        piece = chain.at[h * HALF + my_core]
        return remote(piece, piece, chain_sems.at[0, h], chain_sems.at[1, h], sibling)

    def factors(h):
        three = ring_in.at[pl.ds(0, NY - 1)]
        remote(three, three, ring_sems.at[0, h], ring_sems.at[1, h], (f, o)).wait()
        now = ring_in[h * NY]
        for y in range(1, NY):
            now = now + ring_in[h * NY + y]
        rows, columns = (lax.broadcasted_iota(jnp.int32, (HD, HD), d) for d in range(2))
        eye = jnp.where(rows == columns, 1.0, 0.0)
        inverse = 1.0 / (jnp.sqrt(jnp.sum(now * eye, axis=(0, 1), keepdims=True)) + epsilon)
        now = now * inverse * inverse
        total = None
        for step in range(ITERS):
            factor = first_coeff * eye + second_coeff * now + third_coeff * dot(now, now)
            total = factor if total is None else dot(total, factor)
            if step < ITERS - 1:
                now = dot(factor, dot(now, factor))
        chain[h * HALF + my_core] = total * (gain_factor * math.sqrt(max(D, HD)) * inverse)
        chain_copy(h).start()

    def finish_turns(h, first, last):
        def finish(turn, carry):
            z = (my_z + z_offset(turn)) % NZ
            parts = []
            for j in range(HALF):
                x = nest[h * HALF + j, pl.ds(pl.multiple_of(z * BATCH * SUB, BATCH * SUB), BATCH * SUB), :]
                parts.append(dot_split(x, chain[h * HALF + j]).reshape(BATCH, SUB, HD))
            rows = pl.ds(pl.multiple_of((h * NZ + z) * BATCH * CHUNK, BATCH * CHUNK), BATCH * CHUNK)
            back[rows, :] = jnp.stack(parts, axis=1).reshape(BATCH * CHUNK, HD).astype(jnp.bfloat16)

            def give_row(r, carry):
                x = (my_x + r) % NX
                for kk in range(ROW_SPLIT):
                    e, to_f, to_o = place(z, x, target_k[kk])
                    src, dst = back.at[chunk_of(h * NDEV + e), :], ret_hbm.at[chunk_of(h * NDEV + my_e), :]
                    if kk:
                        remote(src, dst, back_sems.at[0], back_sems.at[1], (to_f, to_o)).start()
                    else:
                        give(src, dst, back_sems.at[0], back_sems.at[1], e, (to_f, to_o))
                return carry

            lax.fori_loop(0, NX, give_row, 0)
            return carry

        lax.fori_loop(first, last, finish, 0)

    grad_in.wait()
    source_in.wait()
    send_turns(0, 0, NZ)
    send_turns(1, 0, 4)
    mom_in.wait()
    absorb_turns(0, 0, NZ)
    pair_copy(0).start()
    send_turns(1, 4, 5)
    ring_start(0)
    send_turns(1, 5, NZ)
    factors(0)
    chain_copy(0).wait()
    finish_turns(0, 0, 4)
    absorb_turns(1, 0, NZ)
    pair_copy(1).start()
    finish_turns(0, 4, 5)
    ring_start(1)
    finish_turns(0, 5, 8)
    factors(1)
    chain_copy(1).wait()
    finish_turns(1, 0, NZ)

    pltpu.make_async_copy(mom, new_hbm, local_sems.at[1]).wait()
    sent = send.at[pl.ds(0, 2 * (NDEV - 1) * CHUNK), :]
    remote(sent, sent, send_sem, send_sem, (f, o)).wait_send()
    remote(sent, sent, back_sems.at[0], back_sems.at[0], (f, o)).wait_send()
    remote(ret_hbm, ret_hbm, back_sems.at[0], back_sems.at[1], (f, o)).wait_recv()


PIECES = 8


def place_kernel(order_ref, ret, new_ref, out_hbm, kept_hbm, wide, out, out_sems):
    pltpu.make_async_copy(new_ref, kept_hbm, out_sems.at[0]).start()

    def widen(index, carry):
        rows = pl.ds(pl.multiple_of(index * 128, 128), 128)
        wide[rows, :] = ret[rows, :].astype(jnp.float32)
        return carry

    lax.fori_loop(0, ROWS // 128, widen, 0, unroll=2)

    columns = order_ref.shape[0] // PIECES
    for i in range(PIECES):

        def column(index, carry):
            p = i * columns + index
            block = order_ref[p]
            j, group = block % BPG, block // BPG
            x, z = (group // 16) * 2 + (group // NZ) % 2, group % NZ
            first = ((j // HALF) * NDEV + (z * NX + x) * ROW_SPLIT) * CHUNK + (j % HALF) * SUB
            tiles = [wide[pl.ds(first + row, ROW_SPLIT, stride=CHUNK), :] for row in range(SUB)]
            out[:, pl.ds(pl.multiple_of(p * HD, HD), HD)] = jnp.concatenate(tiles, axis=0).astype(jnp.bfloat16)
            return carry

        lax.fori_loop(0, columns, column, 0, unroll=8)
        panel = pl.ds(i * columns * HD, columns * HD)
        pltpu.make_async_copy(out.at[:, panel], out_hbm.at[:, panel], out_sems.at[1]).start()

    pltpu.make_async_copy(new_ref, kept_hbm, out_sems.at[0]).wait()
    pltpu.make_async_copy(out, out_hbm, out_sems.at[1]).wait()


def per_device(gradient, momentum, head_order):
    vmem, smem, hbm = (pl.BlockSpec(memory_space=m) for m in (pltpu.VMEM, pltpu.SMEM, pl.ANY))
    returned, new = pl.pallas_call(
        kernel,
        out_shape=(
            jax.ShapeDtypeStruct((ROWS, HD), jnp.bfloat16),
            jax.ShapeDtypeStruct((ROWS, HD), jnp.float32),
        ),
        in_specs=[vmem, hbm, hbm],
        out_specs=(hbm, hbm),
        scratch_shapes=[
            pltpu.VMEM((1, HD), jnp.int32),
            pltpu.SMEM((1, HD), jnp.int32),
            pltpu.VMEM(gradient.shape, jnp.bfloat16),
            pltpu.VMEM((ROWS, HD), jnp.float32),
            pltpu.VMEM((ROWS, HD), jnp.bfloat16),
            pltpu.VMEM((ROWS, HD), jnp.bfloat16),
            pltpu.VMEM((BPG, NDEV * SUB, HD), jnp.float32),
            pltpu.VMEM((ROWS, HD), jnp.bfloat16),
            pltpu.VMEM((HALF, SUB * ROW_SPLIT, HD), jnp.float32),
            pltpu.VMEM((BPG, HD, HD), jnp.float32),
            pltpu.VMEM((2, HD, HD), jnp.float32),
            pltpu.VMEM((2 * NY, HD, HD), jnp.float32),
            pltpu.VMEM((BPG, HD, HD), jnp.float32),
            pltpu.SemaphoreType.DMA,
            pltpu.SemaphoreType.DMA((2, NZ)),
            pltpu.SemaphoreType.DMA((2,)),
            pltpu.SemaphoreType.DMA((2, 2)),
            pltpu.SemaphoreType.DMA((2, 2)),
            pltpu.SemaphoreType.DMA((2, 2)),
            pltpu.SemaphoreType.DMA((4,)),
        ],
        compiler_params=pltpu.CompilerParams(
            collective_id=0, has_side_effects=True, vmem_limit_bytes=45 * 2**20
        ),
    )(head_order[None, :], gradient, momentum.reshape(ROWS, HD))
    placed, kept = pl.pallas_call(
        place_kernel,
        out_shape=(
            jax.ShapeDtypeStruct(gradient.shape, jnp.bfloat16),
            jax.ShapeDtypeStruct((ROWS, HD), jnp.float32),
        ),
        in_specs=[smem, vmem, hbm],
        out_specs=(hbm, hbm),
        scratch_shapes=[
            pltpu.VMEM((ROWS, HD), jnp.float32),
            pltpu.VMEM(gradient.shape, jnp.bfloat16),
            pltpu.SemaphoreType.DMA((2,)),
        ],
        compiler_params=pltpu.CompilerParams(vmem_limit_bytes=16 * 2**20),
    )(head_order, returned, new)
    return (placed, kept.reshape(momentum.shape))


def solution(mesh):
    in_specs = (P(("fsdp", "opt"), None), P("fsdp", "opt", None, None, None), P())
    out_specs = (P(("fsdp", "opt"), None), P("fsdp", "opt", None, None, None))
    return jax.shard_map(
        per_device, mesh=mesh, in_specs=in_specs, out_specs=out_specs, check_vma=False
    )
```

```python
import math

import jax
import jax.numpy as jnp
from jax import lax
from jax.experimental import pallas as pl
from jax.experimental.pallas import tpu as pltpu
from jax.sharding import PartitionSpec as P

D = 16384
HD = 128
BPG = 4
ROW_SPLIT = 8
ITERS = 5
NX, NY, NZ, NCORE = 4, 4, 8, 2
NDEV = NX * NY * NZ * NCORE
SUB = 8
HALF = BPG // 2
CHUNK = SUB * HALF
BATCH = NX * ROW_SPLIT
ROWS = 2 * NDEV * CHUNK

decay_rate = 0.95
first_coeff = 3.4445
second_coeff = -4.775
third_coeff = 2.0315
epsilon = 1e-07
gain_factor = 0.2

MESH = pl.DeviceIdType.MESH
HIGHEST = lax.Precision.HIGHEST


def dot(left, right, left_dim=1):
    return lax.dot_general(
        left, right, (((left_dim,), (0,)), ((), ())), precision=HIGHEST, preferred_element_type=jnp.float32
    )


def split(value):
    high = value.astype(jnp.bfloat16)
    return high, (value - high.astype(jnp.float32)).astype(jnp.bfloat16)


def dot_split(left, right):
    (a, b), (c, d) = split(left), split(right)
    return sum(jnp.dot(u, v, preferred_element_type=jnp.float32) for u, v in ((b, c), (a, d), (a, c)))


def z_offset(turn):
    back = NZ - 1 - turn
    odd = back % 2
    return odd * ((back + 1) // 2) + (1 - odd) * ((NZ - back // 2) % NZ)


def place(z, x, k):
    return (z * NX + x) * ROW_SPLIT + k, ((x % 2) * NZ + z) * ROW_SPLIT + k, x // 2


def chunk_of(index):
    return pl.ds(pl.multiple_of(index * CHUNK, CHUNK), CHUNK)


def kernel(
    order_ref,
    grad_ref,
    mom_hbm,
    ret_hbm,
    new_hbm,
    source_row,
    source_ref,
    mom,
    send,
    recv,
    nest,
    back,
    stage,
    gram,
    pair_in,
    ring_in,
    chain,
    send_sem,
    recv_sem,
    back_sems,
    pair_sems,
    ring_sems,
    chain_sems,
    local_sems,
):
    f, o = lax.axis_index("fsdp"), lax.axis_index("opt")
    my_k = f % ROW_SPLIT
    my_z = (f // ROW_SPLIT) % NZ
    my_x = o * 2 + f // (ROW_SPLIT * NZ)
    my_y, my_core = my_k // 2, my_k % 2
    my_e, _, _ = place(my_z, my_x, my_k)

    mom_in = pltpu.make_async_copy(mom_hbm, mom, local_sems.at[0])
    mom_in.start()

    down, along = (lax.broadcasted_iota(jnp.int32, (HD, HD), d) for d in range(2))
    held = jnp.broadcast_to(order_ref[...], (HD, HD)).T
    source_row[...] = jnp.max(jnp.where(held == along, down, 0), axis=0, keepdims=True)
    source_in = pltpu.make_async_copy(source_row, source_ref, local_sems.at[3])
    source_in.start()

    barrier = pltpu.get_barrier_semaphore()

    leader = (my_k == 0) & (o == 0)
    root = leader & (f == 0)
    groups, members = NX * NZ // 2, 2 * ROW_SPLIT

    def signal(to):
        pl.semaphore_signal(barrier, inc=1, device_id=to, device_id_type=MESH)

    @pl.when(jnp.logical_not(leader))
    def _():
        signal((f - my_k, 0))
        pl.semaphore_wait(barrier, 1)

    @pl.when(leader & (f != 0))
    def _():
        pl.semaphore_wait(barrier, members - 1)
        signal((0, 0))
        pl.semaphore_wait(barrier, 1)

    @pl.when(root)
    def _():
        pl.semaphore_wait(barrier, groups + members - 2)

        def to_leader(group, carry):
            signal((group * ROW_SPLIT, 0))
            return carry

        lax.fori_loop(1, groups, to_leader, 0)

    @pl.when(leader)
    def _():
        def to_member(index, carry):
            signal((f + index // 2, index % 2))
            return carry

        lax.fori_loop(1, members, to_member, 0)

    gram[...] = jnp.zeros_like(gram)

    target_k = [((my_y + kk // 2) % NY) * 2 + (my_core + kk % 2) % 2 for kk in range(ROW_SPLIT)]

    def remote(src, dst, one, two, to):
        return pltpu.make_async_remote_copy(
            src_ref=src, dst_ref=dst, send_sem=one, recv_sem=two, device_id=to, device_id_type=MESH
        )

    def give(src, dst, one, two, e, to):
        @pl.when(e != my_e)
        def _():
            remote(src, dst, one, two, to).start()

        @pl.when(e == my_e)
        def _():
            pltpu.make_async_copy(src, dst, two).start()

    def send_turns(h, first, last):
        def send_group(index, carry):
            turn, r = index // NX, index % NX
            z, x = (my_z + z_offset(turn)) % NZ, (my_x + r) % NX
            group = (x // 2) * 16 + (x % 2) * NZ + z
            for j in range(HALF):
                column = source_ref[0, group * BPG + h * HALF + j] * HD
                stage[j] = grad_ref[:, pl.ds(column, HD)].astype(jnp.float32)
            for kk in range(ROW_SPLIT):
                k = target_k[kk]
                e, to_f, to_o = place(z, x, k)
                parts = [stage[j, pl.ds(k, SUB, stride=ROW_SPLIT), :] for j in range(HALF)]
                send[chunk_of(h * NDEV + e), :] = jnp.concatenate(parts, axis=0).astype(jnp.bfloat16)
                src, dst = send.at[chunk_of(h * NDEV + e), :], recv.at[chunk_of(h * NDEV + my_e), :]
                if kk:
                    remote(src, dst, send_sem, recv_sem.at[h, turn], (to_f, to_o)).start()
                else:
                    give(src, dst, send_sem, recv_sem.at[h, turn], e, (to_f, to_o))
            return carry

        lax.fori_loop(first * NX, last * NX, send_group, 0)

    def absorb_turns(h, first, last):
        def absorb(turn, carry):
            whole = recv.at[pl.ds(0, BATCH * CHUNK), :]
            remote(whole, whole, send_sem, recv_sem.at[h, turn], (f, o)).wait_recv()
            z = (my_z + NZ - z_offset(turn)) % NZ

            def one_chunk(index, carry):
                x, k = index // ROW_SPLIT, index % ROW_SPLIT
                e, from_f, from_o = place(z, x, k)
                value = recv[chunk_of(h * NDEV + e), :].astype(jnp.float32)
                start = (from_f * 2 + from_o) * SUB * BPG
                for j in range(HALF):
                    grad = value[j * SUB : (j + 1) * SUB]
                    rows = pl.ds(start + h * HALF + j, SUB, stride=BPG)
                    new = decay_rate * mom[rows, :] + grad
                    mom[rows, :] = new
                    nest[h * HALF + j, pl.ds(pl.multiple_of(e * SUB, SUB), SUB), :] = grad + decay_rate * new
                return carry

            lax.fori_loop(0, BATCH, one_chunk, 0, unroll=4)
            if h:
                for side in range(2):
                    count = ROW_SPLIT * NCORE * SUB * BPG
                    rows = pl.ds(pl.multiple_of((side * NZ + z) * count, count), count)
                    pltpu.make_async_copy(mom.at[rows, :], new_hbm.at[rows, :], local_sems.at[1]).start()
            for j in range(HALF):
                x = nest[h * HALF + j, pl.ds(pl.multiple_of(z * BATCH * SUB, BATCH * SUB), BATCH * SUB), :]
                gram[h * HALF + j] += dot(x, x, left_dim=0)
            return carry

        lax.fori_loop(first, last, absorb, 0)

    sibling = (f + 1 - 2 * my_core, o)

    def pair_copy(h):
        return remote(
            gram.at[h * HALF + 1 - my_core], pair_in.at[h], pair_sems.at[0, h], pair_sems.at[1, h], sibling
        )

    def ring_start(h):
        pair_copy(h).wait()
        ring_in[h * NY + my_y] = gram[h * HALF + my_core] + pair_in[h]
        for dy in range(1, NY):
            piece = ring_in.at[h * NY + my_y]
            to_f = f - my_k + ((my_y + dy) % NY) * 2 + my_core
            remote(piece, piece, ring_sems.at[0, h], ring_sems.at[1, h], (to_f, o)).start()

    def chain_copy(h):
        piece = chain.at[h * HALF + my_core]
        return remote(piece, piece, chain_sems.at[0, h], chain_sems.at[1, h], sibling)

    def factors(h):
        three = ring_in.at[pl.ds(0, NY - 1)]
        remote(three, three, ring_sems.at[0, h], ring_sems.at[1, h], (f, o)).wait()
        now = ring_in[h * NY]
        for y in range(1, NY):
            now = now + ring_in[h * NY + y]
        rows, columns = (lax.broadcasted_iota(jnp.int32, (HD, HD), d) for d in range(2))
        eye = jnp.where(rows == columns, 1.0, 0.0)
        inverse = 1.0 / (jnp.sqrt(jnp.sum(now * eye, axis=(0, 1), keepdims=True)) + epsilon)
        now = now * inverse * inverse
        total = None
        for step in range(ITERS):
            factor = first_coeff * eye + second_coeff * now + third_coeff * dot(now, now)
            total = factor if total is None else dot(total, factor)
            if step < ITERS - 1:
                now = dot(factor, dot(now, factor))
        chain[h * HALF + my_core] = total * (gain_factor * math.sqrt(max(D, HD)) * inverse)
        chain_copy(h).start()

    def finish_turns(h, first, last):
        def finish(turn, carry):
            z = (my_z + z_offset(turn)) % NZ
            parts = []
            for j in range(HALF):
                x = nest[h * HALF + j, pl.ds(pl.multiple_of(z * BATCH * SUB, BATCH * SUB), BATCH * SUB), :]
                parts.append(dot_split(x, chain[h * HALF + j]).reshape(BATCH, SUB, HD))
            rows = pl.ds(pl.multiple_of((h * NZ + z) * BATCH * CHUNK, BATCH * CHUNK), BATCH * CHUNK)
            back[rows, :] = jnp.stack(parts, axis=1).reshape(BATCH * CHUNK, HD).astype(jnp.bfloat16)

            def give_row(r, carry):
                x = (my_x + r) % NX
                for kk in range(ROW_SPLIT):
                    e, to_f, to_o = place(z, x, target_k[kk])
                    src, dst = back.at[chunk_of(h * NDEV + e), :], ret_hbm.at[chunk_of(h * NDEV + my_e), :]
                    if kk:
                        remote(src, dst, back_sems.at[0], back_sems.at[1], (to_f, to_o)).start()
                    else:
                        give(src, dst, back_sems.at[0], back_sems.at[1], e, (to_f, to_o))
                return carry

            lax.fori_loop(0, NX, give_row, 0)
            return carry

        lax.fori_loop(first, last, finish, 0)

    source_in.wait()
    send_turns(0, 0, NZ)
    send_turns(1, 0, 4)
    mom_in.wait()
    absorb_turns(0, 0, NZ)
    pair_copy(0).start()
    send_turns(1, 4, 5)
    ring_start(0)
    send_turns(1, 5, NZ)
    factors(0)
    chain_copy(0).wait()
    finish_turns(0, 0, 3)
    absorb_turns(1, 0, NZ)
    pair_copy(1).start()
    finish_turns(0, 3, 4)
    ring_start(1)
    finish_turns(0, 4, NZ)
    factors(1)
    chain_copy(1).wait()
    finish_turns(1, 0, NZ)

    pltpu.make_async_copy(mom, new_hbm, local_sems.at[1]).wait()
    sent = send.at[pl.ds(0, 2 * (NDEV - 1) * CHUNK), :]
    remote(sent, sent, send_sem, send_sem, (f, o)).wait_send()
    remote(sent, sent, back_sems.at[0], back_sems.at[0], (f, o)).wait_send()
    remote(ret_hbm, ret_hbm, back_sems.at[0], back_sems.at[1], (f, o)).wait_recv()


PIECES = 8


def place_kernel(order_ref, ret, new_ref, out_hbm, kept_hbm, wide, out, out_sems):
    pltpu.make_async_copy(new_ref, kept_hbm, out_sems.at[0]).start()

    def widen(index, carry):
        rows = pl.ds(pl.multiple_of(index * 128, 128), 128)
        wide[rows, :] = ret[rows, :].astype(jnp.float32)
        return carry

    lax.fori_loop(0, ROWS // 128, widen, 0, unroll=2)

    columns = order_ref.shape[0] // PIECES
    for i in range(PIECES):

        def column(index, carry):
            p = i * columns + index
            block = order_ref[p]
            j, group = block % BPG, block // BPG
            x, z = (group // 16) * 2 + (group // NZ) % 2, group % NZ
            first = ((j // HALF) * NDEV + (z * NX + x) * ROW_SPLIT) * CHUNK + (j % HALF) * SUB
            tiles = [wide[pl.ds(first + row, ROW_SPLIT, stride=CHUNK), :] for row in range(SUB)]
            out[:, pl.ds(pl.multiple_of(p * HD, HD), HD)] = jnp.concatenate(tiles, axis=0).astype(jnp.bfloat16)
            return carry

        lax.fori_loop(0, columns, column, 0, unroll=8)
        panel = pl.ds(i * columns * HD, columns * HD)
        pltpu.make_async_copy(out.at[:, panel], out_hbm.at[:, panel], out_sems.at[1]).start()

    pltpu.make_async_copy(new_ref, kept_hbm, out_sems.at[0]).wait()
    pltpu.make_async_copy(out, out_hbm, out_sems.at[1]).wait()


def per_device(gradient, momentum, head_order):
    vmem, smem, hbm = (pl.BlockSpec(memory_space=m) for m in (pltpu.VMEM, pltpu.SMEM, pl.ANY))
    returned, new = pl.pallas_call(
        kernel,
        out_shape=(
            jax.ShapeDtypeStruct((ROWS, HD), jnp.bfloat16),
            jax.ShapeDtypeStruct((ROWS, HD), jnp.float32),
        ),
        in_specs=[vmem, vmem, hbm],
        out_specs=(hbm, hbm),
        scratch_shapes=[
            pltpu.VMEM((1, HD), jnp.int32),
            pltpu.SMEM((1, HD), jnp.int32),
            pltpu.VMEM((ROWS, HD), jnp.float32),
            pltpu.VMEM((ROWS, HD), jnp.bfloat16),
            pltpu.VMEM((ROWS, HD), jnp.bfloat16),
            pltpu.VMEM((BPG, NDEV * SUB, HD), jnp.float32),
            pltpu.VMEM((ROWS, HD), jnp.bfloat16),
            pltpu.VMEM((HALF, SUB * ROW_SPLIT, HD), jnp.float32),
            pltpu.VMEM((BPG, HD, HD), jnp.float32),
            pltpu.VMEM((2, HD, HD), jnp.float32),
            pltpu.VMEM((2 * NY, HD, HD), jnp.float32),
            pltpu.VMEM((BPG, HD, HD), jnp.float32),
            pltpu.SemaphoreType.DMA,
            pltpu.SemaphoreType.DMA((2, NZ)),
            pltpu.SemaphoreType.DMA((2,)),
            pltpu.SemaphoreType.DMA((2, 2)),
            pltpu.SemaphoreType.DMA((2, 2)),
            pltpu.SemaphoreType.DMA((2, 2)),
            pltpu.SemaphoreType.DMA((4,)),
        ],
        compiler_params=pltpu.CompilerParams(
            collective_id=0, has_side_effects=True, vmem_limit_bytes=45 * 2**20
        ),
    )(head_order[None, :], gradient, momentum.reshape(ROWS, HD))
    placed, kept = pl.pallas_call(
        place_kernel,
        out_shape=(
            jax.ShapeDtypeStruct(gradient.shape, jnp.bfloat16),
            jax.ShapeDtypeStruct((ROWS, HD), jnp.float32),
        ),
        in_specs=[smem, vmem, hbm],
        out_specs=(hbm, hbm),
        scratch_shapes=[
            pltpu.VMEM((ROWS, HD), jnp.float32),
            pltpu.VMEM(gradient.shape, jnp.bfloat16),
            pltpu.SemaphoreType.DMA((2,)),
        ],
        compiler_params=pltpu.CompilerParams(vmem_limit_bytes=16 * 2**20),
    )(head_order, returned, new)
    return (placed, kept.reshape(momentum.shape))


def solution(mesh):
    in_specs = (P(("fsdp", "opt"), None), P("fsdp", "opt", None, None, None), P())
    out_specs = (P(("fsdp", "opt"), None), P("fsdp", "opt", None, None, None))
    return jax.shard_map(
        per_device, mesh=mesh, in_specs=in_specs, out_specs=out_specs, check_vma=False
    )
```
